32 devices in a mesh: dp: 8 (over z, core), seq: 4 (over y, x).
Axes of the slice: x: 2, y: 2, z: 4, core: 2. Of those that a mesh axis runs over, the one named last changes fastest.
Arguments:
- queries: bfloat16 [8, 512, 2048], P('dp', 'seq'), may hold values from -8 to 8
- keys: bfloat16 [8, 512, 2048], P('dp', 'seq'), may hold values from -8 to 8
- values: bfloat16 [8, 512, 2048], P('dp', 'seq'), may hold values from -6 to 6
- out_weight: bfloat16 [2048, 2048], P('dp'), may hold values from -0.125 to 0.125
- cotangent: bfloat16 [8, 512, 2048], P('dp', 'seq'), may hold values from -6 to 6
- block_mask: int32 [8, 4, 4], P('dp'), may hold values from 0 to 1, as said below
Outputs:
- mixed: bfloat16 [8, 512, 2048], P('dp', 'seq')
- grad_queries: bfloat16 [8, 512, 2048], P('dp', 'seq')
- grad_keys: bfloat16 [8, 512, 2048], P('dp', 'seq')
- grad_values: bfloat16 [8, 512, 2048], P('dp', 'seq')
- grad_weight: float32 [2048, 2048], P('dp')
The draws below stay inside these ranges and needn't reach their ends.
Inputs may be any that keep to these rules, and one draw needn't show every extreme that they name: block_mask[b, i, j] is 1 whenever blocks i and j lie in the same view, a view being 8 consecutive blocks (the whole sequence where it has fewer blocks).
All inputs are finite; a program needn't handle non-finite values.
Results may differ from the reference program's by a relative error of at most 0.0075.
Values may be sent and summed in bfloat16 or wider, within the bound.
No kernel may reach another device: no remote copies, remote signals or barrier semaphores. Data moves between devices by JAX's collectives and lax.ppermute only.
A program may use at most 128 MiB of HBM per device.

```python
import math
import jax
import jax.numpy as jnp
from jax import lax

D = 2048
H = 16
DH = 128
BLOCK = 128
VIEW_BLK = 8
SEQ = 512
BATCH = 8
NB = 4


def draw_queries(key, part):
    key = jax.random.fold_in(key, 1)
    sample = jax.random.truncated_normal(key, -3.5, 3.5, (BATCH, SEQ, D), jnp.float32)
    return sample.astype(jnp.bfloat16)


def draw_keys(key, part):
    key = jax.random.fold_in(key, 2)
    sample = jax.random.truncated_normal(key, -3.5, 3.5, (BATCH, SEQ, D), jnp.float32)
    return sample.astype(jnp.bfloat16)


def draw_block_mask(key, part):
    key = jax.random.fold_in(key, 5)
    coins = jax.random.randint(key, (BATCH, NB, NB), 0, 2).astype(jnp.int32)
    views = jnp.arange(NB, dtype=jnp.int32) // VIEW_BLK
    same = (views[:, None] == views[None, :]).astype(jnp.int32)
    return jnp.maximum(coins, same[None, :, :])


def levels(key, extent, pieces, low, largest):
    factor_of, own = 1.0, jax.random.fold_in(key, 6)
    for axis_at, shards_of in pieces:
        heights = jnp.exp(jax.random.uniform(jax.random.fold_in(own, axis_at), (shards_of,), jnp.float32, low / len(pieces), largest / len(pieces)))
        factor_of = factor_of * jnp.repeat(heights, extent[axis_at] // shards_of).reshape([-1 if axis == axis_at else 1 for axis in range(len(extent))])
    return factor_of


def centred(key, extent, scale, most, pieces=(), kind=jnp.bfloat16):
    entries = scale * jax.random.normal(key, extent, jnp.float32)
    if pieces:
        entries = entries * levels(key, extent, pieces, -0.22, 0.18)
    return jnp.clip(entries, -most, most).astype(kind)


def setup_inputs(seed: int = 0) -> dict:
    streams_of = jax.random.split(jax.random.key(seed), 7)
    return {
        "queries": draw_queries(jax.random.fold_in(streams_of[6], 71), 0),
        "keys": draw_keys(jax.random.fold_in(streams_of[6], 71), 0),
        "values": centred(streams_of[2], (BATCH, SEQ, D), 1.0, 6.0, ((0, 8), (1, 4))),
        "out_weight": centred(streams_of[3], (D, D), D ** -0.5, 0.125, ((0, 8),)),
        "cotangent": centred(streams_of[4], (BATCH, SEQ, D), 1.0, 6.0, ((0, 8), (1, 4))),
        "block_mask": draw_block_mask(jax.random.fold_in(streams_of[6], 71), 0),
    }


def head_grads(query_rows, key_rows, value_rows, grad_rows, allowed):
    scale = 1.0 / math.sqrt(DH)
    scores = jnp.dot(query_rows, key_rows.T, preferred_element_type=jnp.float32) * scale
    scores = jnp.where(allowed, scores, -1e+30)
    highest = lax.optimization_barrier(jnp.max(scores, axis=1, keepdims=True))
    log_total = highest + jnp.log(lax.optimization_barrier(jnp.sum(jnp.exp(scores - highest), axis=1, keepdims=True)))
    probs = jnp.exp(scores - log_total)
    rounded = probs.astype(jnp.bfloat16)
    attended = jnp.dot(rounded, value_rows, preferred_element_type=jnp.float32).astype(jnp.bfloat16)
    grad_value = jnp.dot(rounded.T, grad_rows, preferred_element_type=jnp.float32).astype(jnp.bfloat16)
    grad_probs = jnp.dot(grad_rows, value_rows.T, preferred_element_type=jnp.float32)
    delta = lax.optimization_barrier(jnp.sum(probs * grad_probs, axis=1, keepdims=True))
    grad_scores = (probs * (grad_probs - delta) * scale).astype(jnp.bfloat16)
    grad_query = jnp.dot(grad_scores, key_rows, preferred_element_type=jnp.float32).astype(jnp.bfloat16)
    grad_key = jnp.dot(grad_scores.T, query_rows, preferred_element_type=jnp.float32).astype(jnp.bfloat16)
    return (attended, grad_query, grad_key, grad_value)

def split_heads(array):
    return array.reshape(BATCH, SEQ, H, DH).transpose(0, 2, 1, 3).reshape(BATCH * H, SEQ, DH)

def merge_heads(array):
    return array.reshape(BATCH, H, SEQ, DH).transpose(0, 2, 1, 3).reshape(BATCH, SEQ, D)

def reference(queries, keys, values, out_weight, cotangent, block_mask):
    flat_cot = cotangent.reshape(BATCH * SEQ, D)
    grad_attn = jnp.dot(flat_cot, out_weight.T, preferred_element_type=jnp.float32).astype(jnp.bfloat16)
    grad_attn = grad_attn.reshape(BATCH, SEQ, D)
    masks = jnp.repeat(block_mask, H, axis=0)

    def one_head(item):
        query_rows, key_rows, value_rows, grad_rows, mask_rows = item
        allowed = jnp.repeat(jnp.repeat(mask_rows, BLOCK, axis=0), BLOCK, axis=1) > 0
        return head_grads(query_rows, key_rows, value_rows, grad_rows, allowed)
    items = (split_heads(queries), split_heads(keys), split_heads(values), split_heads(grad_attn), masks)
    attended, grad_q, grad_k, grad_v = lax.map(one_head, items)
    attended = merge_heads(attended)
    flat_att = attended.reshape(BATCH * SEQ, D)
    mixed = jnp.dot(flat_att, out_weight, preferred_element_type=jnp.float32).astype(jnp.bfloat16)
    grad_weight = jnp.dot(flat_att.T, flat_cot, preferred_element_type=jnp.float32) / BATCH
    return (mixed.reshape(BATCH, SEQ, D), merge_heads(grad_q), merge_heads(grad_k), merge_heads(grad_v), grad_weight)
```

```python
import functools
import math

import jax
import jax.numpy as jnp
from jax import lax
from jax.experimental import pallas as pl
from jax.experimental.pallas import tpu as pltpu
from jax.sharding import PartitionSpec as P

DH = 128
LOG2E = 1.4426950408889634
F32 = jnp.float32
BF16 = jnp.bfloat16
VMEM_BYTES = 56 * 1024 * 1024


def vmem_specs(count):
    return [pl.BlockSpec(memory_space=pltpu.VMEM)] * count


def params():
    return pltpu.CompilerParams(vmem_limit_bytes=VMEM_BYTES)


def cost(flops, nbytes):
    return pl.CostEstimate(flops=flops, bytes_accessed=nbytes, transcendentals=0)


def head_columns(z, column):
    return pl.ds(pl.multiple_of((4 * z + column) * DH, DH), DH)


def split_kernel(place, query, key, value, *outs):
    for j in range(4):
        column = jnp.bitwise_xor(place[0], j)
        for index, source in enumerate((query, key, value)):
            for z in range(4):
                outs[j][index, :, z * DH : (z + 1) * DH] = source[:, head_columns(z, column)]


def split_heads(place, queries, keys, values):
    tokens, width = queries.shape
    out = jax.ShapeDtypeStruct((3, tokens, width // 4), BF16)
    return pl.pallas_call(
        split_kernel,
        in_specs=[pl.BlockSpec(memory_space=pltpu.SMEM)] + vmem_specs(3),
        out_specs=vmem_specs(4),
        out_shape=[out] * 4,
        compiler_params=params(),
        cost_estimate=cost(0, 12 * tokens * width),
        name="split_heads",
    )(place, queries, keys, values)


def merge_kernel(place, b0, b1, b2, b3, *outs):
    for j, block in enumerate((b0, b1, b2, b3)):
        column = jnp.bitwise_xor(place[0], j)
        for index, target in enumerate(outs):
            for z in range(4):
                target[:, head_columns(z, column)] = block[index, :, z * DH : (z + 1) * DH]


def merge_heads(place, blocks):
    _, tokens, part = blocks[0].shape
    out = jax.ShapeDtypeStruct((tokens, 4 * part), BF16)
    return pl.pallas_call(
        merge_kernel,
        in_specs=[pl.BlockSpec(memory_space=pltpu.SMEM)] + vmem_specs(4),
        out_specs=vmem_specs(3),
        out_shape=[out] * 3,
        compiler_params=params(),
        cost_estimate=cost(0, 48 * tokens * part),
        name="merge_heads",
    )(place, *blocks)


def head_rows(blocks, index, z):
    return jnp.concatenate([b[index, :, z * DH : (z + 1) * DH] for b in blocks], axis=0)


def dot(a, b, a_dim, b_dim):
    return lax.dot_general(a, b, (((a_dim,), (b_dim,)), ((), ())), preferred_element_type=F32)


def scores_kq(place, mask, query, key):
    raw = dot(key, query, 1, 1) * (LOG2E / math.sqrt(DH))
    rows = []
    for r in range(4):
        key_block = jnp.bitwise_xor(place[0], r)
        bias = []
        for p in range(4):
            kept = mask[jnp.bitwise_xor(place[0], p) * 4 + key_block] > 0
            bias.append(jnp.full((1, DH), jnp.where(kept, 0.0, -1e30), F32))
        rows.append(raw[r * DH : (r + 1) * DH] + jnp.concatenate(bias, axis=1))
    return jnp.concatenate(rows, axis=0)


def forward_kernel(place, mask, b0, b1, b2, b3, attended, attended_t, log_total):
    blocks = (b0, b1, b2, b3)
    for z in range(4):
        query, key, value = (head_rows(blocks, i, z) for i in range(3))
        scores = scores_kq(place, mask, query, key)
        highest = jnp.max(scores, axis=0, keepdims=True)
        weights = jnp.exp2(scores - highest)
        total = jnp.sum(weights, axis=0, keepdims=True)
        rounded = (weights * (1.0 / total)).astype(BF16)
        out_t = dot(value, rounded, 0, 0)
        attended_t[z * DH : (z + 1) * DH, :] = out_t.astype(BF16)
        attended[:, z * DH : (z + 1) * DH] = out_t.T.astype(BF16)
        log_total[z : z + 1, :] = highest + jnp.log2(total)


def forward(place, mask, blocks):
    _, tokens, part = blocks[0].shape
    length = 4 * tokens
    return pl.pallas_call(
        forward_kernel,
        in_specs=[pl.BlockSpec(memory_space=pltpu.SMEM)] * 2 + vmem_specs(4),
        out_specs=vmem_specs(3),
        out_shape=[
            jax.ShapeDtypeStruct((length, part), BF16),
            jax.ShapeDtypeStruct((part, length), BF16),
            jax.ShapeDtypeStruct((4, length), F32),
        ],
        compiler_params=params(),
        cost_estimate=cost(4 * length * length * part, 10 * length * part),
        name="forward",
    )(place, mask, *blocks)


def load_slab(place, mine, other, slab, sems):
    core = place[1]
    copies = [
        pltpu.make_async_copy(mine, slab.at[:, pl.ds(pl.multiple_of(core * 64, 64), 64), :], sems.at[0]),
        pltpu.make_async_copy(other, slab.at[:, pl.ds(pl.multiple_of((1 - core) * 64, 64), 64), :], sems.at[1]),
    ]
    for copy in copies:
        copy.start()
    for copy in copies:
        copy.wait()


def mixed_kernel(place, mine, other, attended, send_x, send_y, own, x_right, y_left, slab, sems):
    load_slab(place, mine, other, slab, sems)
    half = slab.shape[2] // 2
    tokens = attended.shape[0] // 4
    for side in range(2):
        for piece in range(2):
            start = side * half + piece * (half // 2)
            here = slice(piece * (half // 2), (piece + 1) * (half // 2))
            total = jnp.zeros((4 * tokens, half // 2), F32)
            for z in range(4):
                total += dot(attended[:, z * DH : (z + 1) * DH], slab[z, :, start : start + half // 2], 1, 0)
            parts = [total[p * tokens : (p + 1) * tokens] for p in range(4)]
            own[:, start : start + half // 2] = parts[0]
            if side == 0:
                send_x[0, :, here] = parts[1].astype(BF16)
                send_x[1, :, here] = parts[3].astype(BF16)
                y_left[:, here] = parts[2]
            else:
                send_y[0, :, here] = parts[2].astype(BF16)
                send_y[1, :, here] = parts[3].astype(BF16)
                x_right[:, here] = parts[1]


def mixed_parts(place, mine, other, attended):
    length, part = attended.shape
    width = mine.shape[2]
    tokens, half = length // 4, width // 2
    return pl.pallas_call(
        mixed_kernel,
        in_specs=[pl.BlockSpec(memory_space=pltpu.SMEM)] + [pl.BlockSpec(memory_space=pl.ANY)] * 2 + vmem_specs(1),
        out_specs=vmem_specs(5),
        out_shape=[
            jax.ShapeDtypeStruct((2, tokens, half), BF16),
            jax.ShapeDtypeStruct((2, tokens, half), BF16),
            jax.ShapeDtypeStruct((tokens, width), F32),
            jax.ShapeDtypeStruct((tokens, half), F32),
            jax.ShapeDtypeStruct((tokens, half), F32),
        ],
        scratch_shapes=[pltpu.VMEM((4, DH, width), BF16), pltpu.SemaphoreType.DMA((2,))],
        compiler_params=params(),
        cost_estimate=cost(2 * length * width * part, 2 * (part * width + length * width)),
        name="mixed_parts",
    )(place, mine, other, attended)


def weight_kernel(place, attended_t, c0, c1, c2, c3, keep, send):
    core = place[1]
    tokens = c0.shape[0]
    for target, half in ((send, 1 - core), (keep, core)):
        rows = [attended_t[pl.ds(pl.multiple_of(z * DH + half * 64, 64), 64), :] for z in range(4)]
        left = jnp.concatenate(rows, axis=0)
        for piece in range(4):
            width = c0.shape[1] // 4
            here = slice(piece * width, (piece + 1) * width)
            total = jnp.zeros((4 * 64, width), F32)
            for p, block in enumerate((c0, c1, c2, c3)):
                total += dot(left[:, p * tokens : (p + 1) * tokens], block[:, here], 1, 0)
            for z in range(4):
                target[z, :, here] = total[z * 64 : (z + 1) * 64].astype(BF16)


def weight_parts(place, attended_t, cot_blocks):
    part, length = attended_t.shape
    width = cot_blocks[0].shape[1]
    out = jax.ShapeDtypeStruct((4, 64, width), BF16)
    return pl.pallas_call(
        weight_kernel,
        in_specs=[pl.BlockSpec(memory_space=pltpu.SMEM)] + vmem_specs(5),
        out_specs=vmem_specs(2),
        out_shape=[out] * 2,
        compiler_params=params(),
        cost_estimate=cost(2 * length * width * part, 2 * (part * width + length * width)),
        name="weight_parts",
    )(place, attended_t, *cot_blocks)


def backward_kernel(place, mask, mine, other, log_total, c0, c1, c2, c3, b0, b1, b2, b3, o0, o1, o2, o3, slab, grads, sems):
    load_slab(place, mine, other, slab, sems)
    cots, blocks, outs = (c0, c1, c2, c3), (b0, b1, b2, b3), (o0, o1, o2, o3)
    tokens = c0.shape[0]
    for pair in range(2):
        rows = jnp.concatenate([slab[2 * pair], slab[2 * pair + 1]], axis=0)
        for p in range(4):
            grads[p * tokens : (p + 1) * tokens, pair * 2 * DH : (pair + 1) * 2 * DH] = dot(
                cots[p][...], rows, 1, 1
            ).astype(BF16)
    scale = 1.0 / math.sqrt(DH)
    for z in range(4):
        query, key, value = (head_rows(blocks, i, z) for i in range(3))
        grad = grads[:, z * DH : (z + 1) * DH]
        probs = jnp.exp2(scores_kq(place, mask, query, key) - log_total[z : z + 1, :])
        grad_value = dot(probs.astype(BF16), grad, 1, 0).astype(BF16)
        grad_probs = dot(value, grad, 1, 1)
        delta = jnp.sum(probs * grad_probs, axis=0, keepdims=True)
        grad_scores = (probs * (grad_probs - delta) * scale).astype(BF16)
        grad_key = dot(grad_scores, query, 1, 0).astype(BF16)
        grad_query = dot(key, grad_scores, 0, 0).T.astype(BF16)
        for index, full in enumerate((grad_query, grad_key, grad_value)):
            for p in range(4):
                outs[p][index, :, z * DH : (z + 1) * DH] = full[p * tokens : (p + 1) * tokens]


def backward(place, mask, mine, other, log_total, cot_blocks, blocks):
    _, tokens, part = blocks[0].shape
    width = mine.shape[2]
    length = 4 * tokens
    smem, hbm = pl.BlockSpec(memory_space=pltpu.SMEM), pl.BlockSpec(memory_space=pl.ANY)
    return pl.pallas_call(
        backward_kernel,
        in_specs=[smem, smem, hbm, hbm] + vmem_specs(9),
        out_specs=vmem_specs(4),
        out_shape=[jax.ShapeDtypeStruct((3, tokens, part), BF16)] * 4,
        scratch_shapes=[
            pltpu.VMEM((4, DH, width), BF16),
            pltpu.VMEM((length, part), BF16),
            pltpu.SemaphoreType.DMA((2,)),
        ],
        compiler_params=params(),
        cost_estimate=cost(2 * length * width * part + 10 * length * length * part, 8 * length * width),
        name="backward",
    )(place, mask, mine, other, log_total, *cot_blocks, *blocks)


def column_shards(queries, keys, values, out_weight, cotangent, block_mask):
    tokens, width = queries.shape[1:]
    column = lax.axis_index("seq")
    rank = lax.axis_index("dp")
    core, z = rank % 2, rank // 2
    place = jnp.stack([column, core, z]).astype(jnp.int32)
    mask = block_mask.reshape(-1)
    cot = cotangent[0]
    far = z >= 2
    inner = (z == 1) | (z == 2)

    def plane(array, flip):
        return lax.ppermute(array, "seq", [(i, i ^ flip) for i in range(4)])

    def swap(array):
        return lax.ppermute(array, "dp", [(i, i ^ 1) for i in range(8)])

    def along(array, pairs):
        return lax.ppermute(array, "dp", [(2 * a + c, 2 * b + c) for a, b in pairs for c in range(2)])

    ends, middle = [(0, 1), (1, 0), (2, 3), (3, 2)], [(1, 2), (2, 1)]
    outward, inward = [(1, 0), (2, 3)], [(0, 1), (3, 2)]

    own, to_x, to_y, to_d = split_heads(place, queries[0], keys[0], values[0])
    blocks = (own, plane(to_x, 1), plane(to_y, 2), plane(to_d, 3))

    start = (column % 2) * DH
    owner = column // 2 == core
    given = swap(lax.dynamic_slice_in_dim(out_weight, start + 64 * (1 - core), 64, 0))
    chunk = jnp.where(owner, lax.dynamic_slice_in_dim(out_weight, start + 64 * core, 64, 0), given)
    near = along(chunk, ends)
    middle_1 = along(chunk, middle)
    middle_2 = along(near, middle)
    third = jnp.where(inner, middle_1, along(middle_1, outward))
    fourth = jnp.where(inner, middle_2, along(middle_2, outward))
    even = z % 2 == 0
    low, high = jnp.where(even, chunk, near), jnp.where(even, near, chunk)
    low_far, high_far = jnp.where(inner == even, fourth, third), jnp.where(inner == even, third, fourth)
    mine = jnp.stack(
        [
            jnp.where(far, low_far, low),
            jnp.where(far, high_far, high),
            jnp.where(far, low, low_far),
            jnp.where(far, high, high_far),
        ]
    )
    other = swap(mine)

    cot_x, cot_y = plane(cot, 1), plane(cot, 2)
    half = tokens // 2
    cot_d = jnp.concatenate([plane(cot_y[:half], 1), plane(cot_x[half:], 2)], axis=0)
    cot_blocks = (cot, cot_x, cot_y, cot_d)

    attended, attended_t, log_total = forward(place, mask, blocks)

    send_x, send_y, mixed_own, x_right, y_left = mixed_parts(place, mine, other, attended)
    got_x, got_y = plane(send_x, 1), plane(send_y, 2)
    got_left = plane((y_left + got_x[1].astype(F32)).astype(BF16), 2)
    got_right = plane((x_right + got_y[1].astype(F32)).astype(BF16), 1)
    mixed = jnp.concatenate(
        [
            mixed_own[:, : width // 2] + got_x[0].astype(F32) + got_left.astype(F32),
            mixed_own[:, width // 2 :] + got_y[0].astype(F32) + got_right.astype(F32),
        ],
        axis=1,
    ).astype(BF16)

    keep, send = weight_parts(place, attended_t, cot_blocks)
    both = (keep.astype(F32) + swap(send).astype(F32)).astype(BF16)
    both = jnp.where(far, both[::-1], both)
    got3 = along(both[3], inward)
    got21 = along(both[1:3], inward)
    cross_far = along(both[3] + got3, middle)
    cross_near = along(both[2] + got21[1], middle)
    to_end = along(both[0] + cross_far, outward)
    summed = jnp.where(inner, both[1] + got21[0] + cross_near, both[0] + to_end)
    sum_x, sum_y = plane(summed, 1), plane(summed, 2)
    sum_d = jnp.concatenate([plane(sum_y[:32], 1), plane(sum_x[32:], 2)], axis=0)
    high_x, high_y = column % 2 == 1, column >= 2
    row = (jnp.where(high_x, sum_x, summed), jnp.where(high_x, summed, sum_x))
    cross = (jnp.where(high_x, sum_d, sum_y), jnp.where(high_x, sum_y, sum_d))
    first = jnp.stack([jnp.where(high_y, cross[i], row[i]) for i in range(2)])
    second = jnp.stack([jnp.where(high_y, row[i], cross[i]) for i in range(2)])
    is_one = core == 1
    stay = jnp.where(is_one, second, first)
    arrive = swap(jnp.where(is_one, first, second))
    batch = lax.axis_size("dp")
    grad_weight = (
        jnp.stack([jnp.where(is_one, arrive, stay), jnp.where(is_one, stay, arrive)], axis=1)
        .reshape(out_weight.shape)
        .astype(F32)
        / batch
    )

    outs = backward(place, mask, mine, other, log_total, cot_blocks, blocks)
    grads = merge_heads(place, (outs[0], plane(outs[1], 1), plane(outs[2], 2), plane(outs[3], 3)))
    return (mixed[None],) + tuple(g[None] for g in grads) + (grad_weight,)


def attend(query_heads, key_heads, value_heads, grad_heads, block_mask):
    batch, length, width = query_heads.shape
    heads = width // DH
    shape_split = (batch, length, heads, DH)
    query_split = query_heads.reshape(shape_split)
    key_split = key_heads.reshape(shape_split)
    value_split = value_heads.reshape(shape_split)
    grad_split = grad_heads.reshape(shape_split)
    block = length // block_mask.shape[2]
    rows_step = min(512, length)
    scale = 1.0 / math.sqrt(DH)

    def step(carry, index):
        key_total, value_total = carry
        start = index * rows_step
        query_part = lax.dynamic_slice_in_dim(query_split, start, rows_step, 1)
        grad_part = lax.dynamic_slice_in_dim(grad_split, start, rows_step, 1)
        mask_part = lax.dynamic_slice_in_dim(block_mask, start // block, rows_step // block, 1)
        allowed = jnp.repeat(jnp.repeat(mask_part, block, axis=1), block, axis=2) > 0
        scores = (
            jnp.einsum("bqhd,bkhd->bhqk", query_part, key_split, preferred_element_type=jnp.float32)
            * scale
        )
        scores = jnp.where(allowed[:, None], scores, -1e30)
        highest = jnp.max(scores, axis=3, keepdims=True)
        log_total = highest + jnp.log(jnp.sum(jnp.exp(scores - highest), axis=3, keepdims=True))
        probs = jnp.exp(scores - log_total)
        rounded = probs.astype(jnp.bfloat16)
        attended = jnp.einsum(
            "bhqk,bkhd->bqhd", rounded, value_split, preferred_element_type=jnp.float32
        ).astype(jnp.bfloat16)
        value_total = value_total + jnp.einsum(
            "bhqk,bqhd->bkhd", rounded, grad_part, preferred_element_type=jnp.float32
        )
        grad_probs = jnp.einsum(
            "bqhd,bkhd->bhqk", grad_part, value_split, preferred_element_type=jnp.float32
        )
        delta = jnp.sum(probs * grad_probs, axis=3, keepdims=True)
        grad_scores = (probs * (grad_probs - delta) * scale).astype(jnp.bfloat16)
        grad_query = jnp.einsum(
            "bhqk,bkhd->bqhd", grad_scores, key_split, preferred_element_type=jnp.float32
        ).astype(jnp.bfloat16)
        key_total = key_total + jnp.einsum(
            "bhqk,bqhd->bkhd", grad_scores, query_part, preferred_element_type=jnp.float32
        )
        return ((key_total, value_total), (attended, grad_query))

    zeros = jnp.zeros(shape_split, jnp.float32)
    totals, pieces = lax.scan(
        step, (zeros, zeros), jnp.arange(length // rows_step, dtype=jnp.int32)
    )

    def joined(parts):
        return jnp.moveaxis(parts, 0, 1).reshape(batch, length, width)

    grad_key = totals[0].astype(jnp.bfloat16).reshape(batch, length, width)
    grad_value = totals[1].astype(jnp.bfloat16).reshape(batch, length, width)
    return (joined(pieces[0]), joined(pieces[1]), grad_key, grad_value)


def general_shards(queries, keys, values, out_weight, cotangent, block_mask):
    batch, tokens, width = queries.shape
    query_heads, key_heads, value_heads = (
        lax.all_to_all(queries, "seq", split_axis=2, concat_axis=1, tiled=True),
        lax.all_to_all(keys, "seq", split_axis=2, concat_axis=1, tiled=True),
        lax.all_to_all(values, "seq", split_axis=2, concat_axis=1, tiled=True),
    )
    weight_full = lax.all_gather(out_weight, "dp", axis=0, tiled=True)
    flat_cot = cotangent.reshape(batch * tokens, width)
    grad_attn = lax.dot_general(
        flat_cot, weight_full, (((1,), (1,)), ((), ())), preferred_element_type=jnp.float32
    )
    grad_attn = grad_attn.astype(jnp.bfloat16).reshape(batch, tokens, width)
    grad_heads = lax.all_to_all(grad_attn, "seq", split_axis=2, concat_axis=1, tiled=True)
    attended_heads, grad_q_heads, grad_k_heads, grad_v_heads = attend(
        query_heads, key_heads, value_heads, grad_heads, block_mask
    )
    attended, grad_queries, grad_keys, grad_values = (
        lax.all_to_all(attended_heads, "seq", split_axis=1, concat_axis=2, tiled=True),
        lax.all_to_all(grad_q_heads, "seq", split_axis=1, concat_axis=2, tiled=True),
        lax.all_to_all(grad_k_heads, "seq", split_axis=1, concat_axis=2, tiled=True),
        lax.all_to_all(grad_v_heads, "seq", split_axis=1, concat_axis=2, tiled=True),
    )
    flat_att = attended.reshape(batch * tokens, width)
    mixed = (
        jnp.dot(flat_att, weight_full, preferred_element_type=jnp.float32)
        .astype(jnp.bfloat16)
        .reshape(batch, tokens, width)
    )
    partial_grad = lax.psum_scatter(
        lax.dot_general(
            flat_att, flat_cot, (((0,), (0,)), ((), ())), preferred_element_type=jnp.float32
        ),
        "dp",
        scatter_dimension=0,
        tiled=True,
    )
    summed = lax.psum(partial_grad, "seq")
    grad_weight = summed / (batch * lax.axis_size("dp"))
    return (mixed, grad_queries, grad_keys, grad_values, grad_weight)


def fits_columns(mesh, queries, out_weight, block_mask):
    batch, length, width = queries
    return (
        mesh.shape["dp"] == 8
        and mesh.shape["seq"] == 4
        and batch == 8
        and length == 4 * DH
        and width == 16 * DH
        and out_weight == (width, width)
        and block_mask == (batch, 4, 4)
    )


def solution(mesh):
    placed = (
        P("dp", "seq", None),
        P("dp", "seq", None),
        P("dp", "seq", None),
        P("dp", None),
        P("dp", "seq", None),
        P("dp", None, None),
    )

    def program(queries, keys, values, out_weight, cotangent, block_mask):
        fits = fits_columns(mesh, queries.shape, out_weight.shape, block_mask.shape)
        return jax.shard_map(
            column_shards if fits else general_shards,
            mesh=mesh,
            in_specs=placed,
            out_specs=(
                P("dp", "seq", None),
                P("dp", "seq", None),
                P("dp", "seq", None),
                P("dp", "seq", None),
                P("dp", None),
            ),
            check_vma=False,
        )(queries, keys, values, out_weight, cotangent, block_mask)

    return program
```

```python
import math

import jax
import jax.numpy as jnp
from jax import lax
from jax.experimental import pallas as pl
from jax.experimental.pallas import tpu as pltpu
from jax.sharding import PartitionSpec as P

DH = 128
HALF = DH // 2
LOG2E = 1.4426950408889634
F32 = jnp.float32
BF16 = jnp.bfloat16
VMEM_BYTES = 56 * 1024 * 1024


SMEM = pl.BlockSpec(memory_space=pltpu.SMEM)
VMEM = pl.BlockSpec(memory_space=pltpu.VMEM)
HBM = pl.BlockSpec(memory_space=pl.ANY)


def call(kernel, name, operands, in_specs, out_shape, out_specs, scratch=(), flops=0, after=()):
    extra = len(after)

    def body(*refs):
        kernel(*refs[: len(operands)], *refs[len(operands) + extra :])

    nbytes = sum(x.size * x.dtype.itemsize for x in (*operands, *out_shape))
    return pl.pallas_call(
        body,
        in_specs=list(in_specs) + [HBM] * extra,
        out_specs=list(out_specs),
        out_shape=list(out_shape),
        scratch_shapes=list(scratch),
        compiler_params=pltpu.CompilerParams(vmem_limit_bytes=VMEM_BYTES),
        cost_estimate=pl.CostEstimate(flops=flops, bytes_accessed=nbytes, transcendentals=0),
        name=name,
    )(*operands, *after)


def run_copies(pairs, sems, first=0):
    copies = [pltpu.make_async_copy(s, d, sems.at[first + i]) for i, (s, d) in enumerate(pairs)]
    for copy in copies:
        copy.start()
    return copies


def head_columns(place, block, head):
    column = 4 * jnp.bitwise_xor(place[2], head) + jnp.bitwise_xor(place[0], block)
    return pl.ds(pl.multiple_of(column * DH, DH), DH)


def split_kernel(place, query, key, value, o0, o1, o2, o3):
    for j, out in enumerate((o0, o1, o2, o3)):
        for index, source in enumerate((query, key, value)):
            for h in range(4):
                out[index, :, h * DH : (h + 1) * DH] = source[:, head_columns(place, j, h)]


def split_heads(place, queries, keys, values):
    tokens, width = queries.shape
    out = jax.ShapeDtypeStruct((3, tokens, width // 4), BF16)
    return call(split_kernel, "split_heads", (place, queries, keys, values), [SMEM] + [VMEM] * 3, [out] * 4, [VMEM] * 4)


def merge_kernel(place, b0, b1, b2, b3, *outs):
    for j, block in enumerate((b0, b1, b2, b3)):
        for index, target in enumerate(outs):
            for h in range(4):
                target[:, head_columns(place, j, h)] = block[index, :, h * DH : (h + 1) * DH]


def merge_heads(place, blocks):
    _, tokens, part = blocks[0].shape
    out = jax.ShapeDtypeStruct((tokens, 4 * part), BF16)
    return call(merge_kernel, "merge_heads", (place, *blocks), [SMEM] + [VMEM] * 4, [out] * 3, [VMEM] * 3)


def dot(a, b, a_dim, b_dim):
    return lax.dot_general(a, b, (((a_dim,), (b_dim,)), ((), ())), preferred_element_type=F32)


def load_blocks(blocks, rows, sems, first):
    tokens = blocks[0].shape[1]
    return run_copies([(b, rows.at[:, pl.ds(p * tokens, tokens), :]) for p, b in enumerate(blocks)], sems, first)


def load_cots(blocks, rows, sems, first):
    tokens = blocks[0].shape[0]
    return run_copies([(b, rows.at[pl.ds(p * tokens, tokens), :]) for p, b in enumerate(blocks)], sems, first)


def load_slab(place, mine, other, slab, sems, first):
    pairs = []
    for h in range(4):
        for source, half in ((mine[h], place[1]), (other[h], 1 - place[1])):
            pairs.append((source, slab.at[pl.ds(pl.multiple_of(h * DH + half * HALF, HALF), HALF), :]))
    return run_copies(pairs, sems, first)


def bias_rows(place, mask):
    rows = []
    for r in range(4):
        key_block = jnp.bitwise_xor(place[0], r)
        row = []
        for p in range(4):
            kept = mask[jnp.bitwise_xor(place[0], p) * 4 + key_block] > 0
            row.append(jnp.full((1, DH), jnp.where(kept, 0.0, -1e30), F32))
        rows.append(jnp.concatenate(row, axis=1))
    return rows


def scores_kq(bias, query, key):
    raw = dot(key, query, 1, 1) * (LOG2E / math.sqrt(DH))
    return jnp.concatenate([raw[r * DH : (r + 1) * DH] + bias[r] for r in range(4)], axis=0)


def forward_kernel(place, mask, b0, b1, b2, b3, attended, attended_t, log_total, qkv, sems):
    copies = load_blocks((b0, b1, b2, b3), qkv, sems, 0)
    bias = bias_rows(place, mask)
    for copy in copies:
        copy.wait()
    for h in range(4):
        here = slice(h * DH, (h + 1) * DH)
        scores = scores_kq(bias, qkv[0, :, here], qkv[1, :, here])
        highest = jnp.max(scores, axis=0, keepdims=True)
        weights = jnp.exp2(scores - highest)
        total = jnp.sum(weights, axis=0, keepdims=True)
        rounded = (weights * (1.0 / total)).astype(BF16)
        out_t = dot(qkv[2, :, here], rounded, 0, 0).astype(BF16)
        attended_t[here, :] = out_t
        attended[:, here] = out_t.T
        log_total[h : h + 1, :] = highest + jnp.log2(total)


def forward(place, mask, blocks, after=()):
    _, tokens, part = blocks[0].shape
    length = 4 * tokens
    return call(
        forward_kernel,
        "forward",
        (place, mask, *blocks),
        [SMEM] * 2 + [HBM] * 4,
        [
            jax.ShapeDtypeStruct((length, part), BF16),
            jax.ShapeDtypeStruct((part, length), BF16),
            jax.ShapeDtypeStruct((4, length), F32),
        ],
        [VMEM] * 3,
        [pltpu.VMEM((3, length, part), BF16), pltpu.SemaphoreType.DMA((4,))],
        flops=4 * length * length * part,
        after=after,
    )


def mixed_kernel(place, m0, m1, m2, m3, r0, r1, r2, r3, attended, send_x, send_y, own, x_right, y_left, slab, sems):
    copies = load_slab(place, (m0, m1, m2, m3), (r0, r1, r2, r3), slab, sems, 0)
    for copy in copies:
        copy.wait()
    tokens = attended.shape[0] // 4
    step = slab.shape[1] // 4
    for piece in range(4):
        columns = slice(piece * step, (piece + 1) * step)
        here = slice((piece % 2) * step, (piece % 2 + 1) * step)
        total = dot(attended[...], slab[:, columns], 1, 0)
        parts = [total[p * tokens : (p + 1) * tokens] for p in range(4)]
        own[:, columns] = parts[0].astype(BF16)
        if piece < 2:
            send_x[0, :, here] = parts[1].astype(BF16)
            send_x[1, :, here] = parts[3].astype(BF16)
            y_left[:, here] = parts[2].astype(BF16)
        else:
            send_y[0, :, here] = parts[2].astype(BF16)
            send_y[1, :, here] = parts[3].astype(BF16)
            x_right[:, here] = parts[1].astype(BF16)


def mixed_parts(place, mine, other, attended, after=()):
    length, part = attended.shape
    width = mine[0].shape[1]
    tokens, half = length // 4, width // 2
    return call(
        mixed_kernel,
        "mixed_parts",
        (place, *mine, *other, attended),
        [SMEM] + [HBM] * 8 + [VMEM],
        [
            jax.ShapeDtypeStruct((2, tokens, half), BF16),
            jax.ShapeDtypeStruct((2, tokens, half), BF16),
            jax.ShapeDtypeStruct((tokens, width), BF16),
            jax.ShapeDtypeStruct((tokens, half), BF16),
            jax.ShapeDtypeStruct((tokens, half), BF16),
        ],
        [VMEM] * 5,
        [pltpu.VMEM((part, width), BF16), pltpu.SemaphoreType.DMA((8,))],
        flops=2 * length * width * part,
        after=after,
    )


def weight_kernel(place, attended_t, c0, c1, c2, c3, keep, send, cots, sems):
    copies = load_cots((c0, c1, c2, c3), cots, sems, 0)
    core = place[1]
    rows = []
    for half in (1 - core, core):
        for h in range(4):
            rows.append(attended_t[pl.ds(pl.multiple_of(h * DH + half * HALF, HALF), HALF), :])
    left = jnp.concatenate(rows, axis=0)
    for copy in copies:
        copy.wait()
    step = cots.shape[1] // 4
    for piece in range(4):
        columns = slice(piece * step, (piece + 1) * step)
        total = dot(left, cots[:, columns], 1, 0).astype(BF16)
        for h in range(4):
            send[h, :, columns] = total[h * HALF : (h + 1) * HALF]
            keep[h, :, columns] = total[(4 + h) * HALF : (5 + h) * HALF]


def weight_parts(place, attended_t, cot_blocks, after=()):
    part, length = attended_t.shape
    width = cot_blocks[0].shape[1]
    out = jax.ShapeDtypeStruct((4, HALF, width), BF16)
    return call(
        weight_kernel,
        "weight_parts",
        (place, attended_t, *cot_blocks),
        [SMEM, VMEM] + [HBM] * 4,
        [out] * 2,
        [VMEM] * 2,
        [pltpu.VMEM((length, width), BF16), pltpu.SemaphoreType.DMA((4,))],
        flops=2 * length * width * part,
        after=after,
    )


def add_kernel(keep, got, *outs):
    for h, out in enumerate(outs):
        out[...] = (keep[h].astype(F32) + got[h].astype(F32)).astype(BF16)


def add_cores(keep, got):
    out = jax.ShapeDtypeStruct(keep.shape[1:], BF16)
    return call(add_kernel, "add_cores", (keep, got), [VMEM] * 2, [out] * 4, [VMEM] * 4)


def weight_out_kernel(place, p0, p1, p2, p3, out):
    for k, piece in enumerate((p0, p1, p2, p3)):
        head = jnp.bitwise_xor(place[0] % 2, k % 2)
        half = jnp.bitwise_xor(jnp.bitwise_xor(place[1], place[0] // 2), k // 2)
        start = pl.multiple_of(head * DH + half * HALF, HALF)
        out[pl.ds(start, HALF), :] = piece[...].astype(F32) * 0.125


def weight_out(place, pieces):
    rows, width = pieces[0].shape
    out = jax.ShapeDtypeStruct((4 * rows, width), F32)
    return call(weight_out_kernel, "weight_out", (place, *pieces), [SMEM] + [VMEM] * 4, [out], [VMEM])[0]


def backward_kernel(
    place, mask, m0, m1, m2, m3, r0, r1, r2, r3, log_total, c0, c1, c2, c3, b0, b1, b2, b3,
    o0, o1, o2, o3, slab, cots, qkv, grads, sems,
):
    slab_copies = load_slab(place, (m0, m1, m2, m3), (r0, r1, r2, r3), slab, sems, 0)
    cot_copies = load_cots((c0, c1, c2, c3), cots, sems, 8)
    qkv_copies = load_blocks((b0, b1, b2, b3), qkv, sems, 12)
    outs = (o0, o1, o2, o3)
    tokens = c0.shape[0]
    for copy in slab_copies + cot_copies:
        copy.wait()
    for pair in range(2):
        rows = slice(pair * 2 * DH, (pair + 1) * 2 * DH)
        grads[:, rows] = dot(cots[...], slab[rows, :], 1, 1).astype(BF16)
    for copy in qkv_copies:
        copy.wait()
    scale = 1.0 / math.sqrt(DH)
    bias = bias_rows(place, mask)
    for h in range(4):
        here = slice(h * DH, (h + 1) * DH)
        query, key, value, grad = qkv[0, :, here], qkv[1, :, here], qkv[2, :, here], grads[:, here]
        probs = jnp.exp2(scores_kq(bias, query, key) - log_total[h : h + 1, :])
        grad_value = dot(probs.astype(BF16), grad, 1, 0).astype(BF16)
        grad_probs = dot(value, grad, 1, 1)
        delta = jnp.sum(probs * grad_probs, axis=0, keepdims=True)
        grad_scores = (probs * (grad_probs - delta) * scale).astype(BF16)
        grad_key = dot(grad_scores, query, 1, 0).astype(BF16)
        grad_query = dot(key, grad_scores, 0, 0).astype(BF16).T
        for index, full in enumerate((grad_query, grad_key, grad_value)):
            for p in range(4):
                outs[p][index, :, here] = full[p * tokens : (p + 1) * tokens]


def backward(place, mask, mine, other, log_total, cot_blocks, blocks, after=()):
    _, tokens, part = blocks[0].shape
    width = mine[0].shape[1]
    length = 4 * tokens
    return call(
        backward_kernel,
        "backward",
        (place, mask, *mine, *other, log_total, *cot_blocks, *blocks),
        [SMEM] * 2 + [HBM] * 8 + [VMEM] + [HBM] * 8,
        [jax.ShapeDtypeStruct((3, tokens, part), BF16)] * 4,
        [VMEM] * 4,
        [
            pltpu.VMEM((part, width), BF16),
            pltpu.VMEM((length, width), BF16),
            pltpu.VMEM((3, length, part), BF16),
            pltpu.VMEM((length, part), BF16),
            pltpu.SemaphoreType.DMA((16,)),
        ],
        flops=2 * length * width * part + 10 * length * length * part,
        after=after,
    )


def column_shards(queries, keys, values, out_weight, cotangent, block_mask):
    tokens, width = queries.shape[1:]
    column = lax.axis_index("seq")
    rank = lax.axis_index("dp")
    core, z = rank % 2, rank // 2
    place = jnp.stack([column, core, z]).astype(jnp.int32)
    mask = block_mask.reshape(-1)
    cot = cotangent[0]

    def plane(array, flip):
        return lax.ppermute(array, "seq", [(i, i ^ flip) for i in range(4)])

    def swap(array):
        return lax.ppermute(array, "dp", [(i, i ^ 1) for i in range(8)])

    def along(array, flip):
        return lax.ppermute(array, "dp", [(i, i ^ (2 * flip)) for i in range(8)])

    own, to_x, to_y, to_d = split_heads(place, queries[0], keys[0], values[0])
    blocks = (own, plane(to_x, 1), plane(to_y, 2), plane(to_d, 3))

    cot_x, cot_y = plane(cot, 1), plane(cot, 2)
    half = tokens // 2
    cot_d = jnp.concatenate([plane(cot_y[:half], 1), plane(cot_x[half:], 2)], axis=0)
    cot_blocks = (cot, cot_x, cot_y, cot_d)

    start = (column % 2) * DH
    owner = column // 2 == core
    given = swap(lax.dynamic_slice_in_dim(out_weight, start + HALF * (1 - core), HALF, 0))
    chunk = jnp.where(owner, lax.dynamic_slice_in_dim(out_weight, start + HALF * core, HALF, 0), given)
    mine = (chunk, along(chunk, 1), along(chunk, 2), along(chunk, 3))
    other = tuple(swap(m) for m in mine)

    attended, attended_t, log_total = forward(place, mask, blocks)

    send_x, send_y, mixed_own, x_right, y_left = mixed_parts(place, mine, other, attended)
    got_x, got_y = plane(send_x, 1), plane(send_y, 2)
    got_left = plane((y_left.astype(F32) + got_x[1].astype(F32)).astype(BF16), 2)
    got_right = plane((x_right.astype(F32) + got_y[1].astype(F32)).astype(BF16), 1)
    mixed = jnp.concatenate(
        [
            mixed_own[:, : width // 2].astype(F32) + got_x[0].astype(F32) + got_left.astype(F32),
            mixed_own[:, width // 2 :].astype(F32) + got_y[0].astype(F32) + got_right.astype(F32),
        ],
        axis=1,
    ).astype(BF16)

    keep, send = weight_parts(place, attended_t, cot_blocks, after=(send_x,))
    s0, s1, s2, s3 = add_cores(keep, swap(send))
    got = [along(s, flip).astype(F32) for flip, s in ((1, s1), (2, s2), (3, s3))]
    summed = (s0.astype(F32) + got[0] + got[1] + got[2]).astype(BF16)
    pieces = []
    for k in range(4):
        pairs = []
        for plane_at in range(4):
            for c in range(2):
                for t in range(4):
                    to_core, to_column = t // 2, t ^ (2 * c) ^ k
                    pairs.append(((2 * plane_at + c) * 4 + t, (2 * plane_at + to_core) * 4 + to_column))
        pieces.append(lax.ppermute(summed, ("dp", "seq"), pairs))
    grad_weight = weight_out(place, pieces)

    outs = backward(place, mask, mine, other, log_total, cot_blocks, blocks, after=(keep,))
    grads = merge_heads(place, (outs[0], plane(outs[1], 1), plane(outs[2], 2), plane(outs[3], 3)))
    return (mixed[None],) + tuple(g[None] for g in grads) + (grad_weight,)


def attend(query_heads, key_heads, value_heads, grad_heads, block_mask):
    batch, length, width = query_heads.shape
    heads = width // DH
    shape_split = (batch, length, heads, DH)
    query_split = query_heads.reshape(shape_split)
    key_split = key_heads.reshape(shape_split)
    value_split = value_heads.reshape(shape_split)
    grad_split = grad_heads.reshape(shape_split)
    block = length // block_mask.shape[2]
    rows_step = min(512, length)
    scale = 1.0 / math.sqrt(DH)

    def step(carry, index):
        key_total, value_total = carry
        start = index * rows_step
        query_part = lax.dynamic_slice_in_dim(query_split, start, rows_step, 1)
        grad_part = lax.dynamic_slice_in_dim(grad_split, start, rows_step, 1)
        mask_part = lax.dynamic_slice_in_dim(block_mask, start // block, rows_step // block, 1)
        allowed = jnp.repeat(jnp.repeat(mask_part, block, axis=1), block, axis=2) > 0
        scores = (
            jnp.einsum("bqhd,bkhd->bhqk", query_part, key_split, preferred_element_type=jnp.float32)
            * scale
        )
        scores = jnp.where(allowed[:, None], scores, -1e30)
        highest = jnp.max(scores, axis=3, keepdims=True)
        log_total = highest + jnp.log(jnp.sum(jnp.exp(scores - highest), axis=3, keepdims=True))
        probs = jnp.exp(scores - log_total)
        rounded = probs.astype(jnp.bfloat16)
        attended = jnp.einsum(
            "bhqk,bkhd->bqhd", rounded, value_split, preferred_element_type=jnp.float32
        ).astype(jnp.bfloat16)
        value_total = value_total + jnp.einsum(
            "bhqk,bqhd->bkhd", rounded, grad_part, preferred_element_type=jnp.float32
        )
        grad_probs = jnp.einsum(
            "bqhd,bkhd->bhqk", grad_part, value_split, preferred_element_type=jnp.float32
        )
        delta = jnp.sum(probs * grad_probs, axis=3, keepdims=True)
        grad_scores = (probs * (grad_probs - delta) * scale).astype(jnp.bfloat16)
        grad_query = jnp.einsum(
            "bhqk,bkhd->bqhd", grad_scores, key_split, preferred_element_type=jnp.float32
        ).astype(jnp.bfloat16)
        key_total = key_total + jnp.einsum(
            "bhqk,bqhd->bkhd", grad_scores, query_part, preferred_element_type=jnp.float32
        )
        return ((key_total, value_total), (attended, grad_query))

    zeros = jnp.zeros(shape_split, jnp.float32)
    totals, pieces = lax.scan(
        step, (zeros, zeros), jnp.arange(length // rows_step, dtype=jnp.int32)
    )

    def joined(parts):
        return jnp.moveaxis(parts, 0, 1).reshape(batch, length, width)

    grad_key = totals[0].astype(jnp.bfloat16).reshape(batch, length, width)
    grad_value = totals[1].astype(jnp.bfloat16).reshape(batch, length, width)
    return (joined(pieces[0]), joined(pieces[1]), grad_key, grad_value)


def general_shards(queries, keys, values, out_weight, cotangent, block_mask):
    batch, tokens, width = queries.shape
    query_heads, key_heads, value_heads = (
        lax.all_to_all(queries, "seq", split_axis=2, concat_axis=1, tiled=True),
        lax.all_to_all(keys, "seq", split_axis=2, concat_axis=1, tiled=True),
        lax.all_to_all(values, "seq", split_axis=2, concat_axis=1, tiled=True),
    )
    weight_full = lax.all_gather(out_weight, "dp", axis=0, tiled=True)
    flat_cot = cotangent.reshape(batch * tokens, width)
    grad_attn = lax.dot_general(
        flat_cot, weight_full, (((1,), (1,)), ((), ())), preferred_element_type=jnp.float32
    )
    grad_attn = grad_attn.astype(jnp.bfloat16).reshape(batch, tokens, width)
    grad_heads = lax.all_to_all(grad_attn, "seq", split_axis=2, concat_axis=1, tiled=True)
    attended_heads, grad_q_heads, grad_k_heads, grad_v_heads = attend(
        query_heads, key_heads, value_heads, grad_heads, block_mask
    )
    attended, grad_queries, grad_keys, grad_values = (
        lax.all_to_all(attended_heads, "seq", split_axis=1, concat_axis=2, tiled=True),
        lax.all_to_all(grad_q_heads, "seq", split_axis=1, concat_axis=2, tiled=True),
        lax.all_to_all(grad_k_heads, "seq", split_axis=1, concat_axis=2, tiled=True),
        lax.all_to_all(grad_v_heads, "seq", split_axis=1, concat_axis=2, tiled=True),
    )
    flat_att = attended.reshape(batch * tokens, width)
    mixed = (
        jnp.dot(flat_att, weight_full, preferred_element_type=jnp.float32)
        .astype(jnp.bfloat16)
        .reshape(batch, tokens, width)
    )
    partial_grad = lax.psum_scatter(
        lax.dot_general(
            flat_att, flat_cot, (((0,), (0,)), ((), ())), preferred_element_type=jnp.float32
        ),
        "dp",
        scatter_dimension=0,
        tiled=True,
    )
    summed = lax.psum(partial_grad, "seq")
    grad_weight = summed / (batch * lax.axis_size("dp"))
    return (mixed, grad_queries, grad_keys, grad_values, grad_weight)


def fits_columns(mesh, queries, out_weight, block_mask):
    batch, length, width = queries
    return (
        mesh.shape["dp"] == 8
        and mesh.shape["seq"] == 4
        and batch == 8
        and length == 4 * DH
        and width == 16 * DH
        and out_weight == (width, width)
        and block_mask == (batch, 4, 4)
    )


def solution(mesh):
    placed = (
        P("dp", "seq", None),
        P("dp", "seq", None),
        P("dp", "seq", None),
        P("dp", None),
        P("dp", "seq", None),
        P("dp", None, None),
    )

    def program(queries, keys, values, out_weight, cotangent, block_mask):
        fits = fits_columns(mesh, queries.shape, out_weight.shape, block_mask.shape)
        return jax.shard_map(
            column_shards if fits else general_shards,
            mesh=mesh,
            in_specs=placed,
            out_specs=(
                P("dp", "seq", None),
                P("dp", "seq", None),
                P("dp", "seq", None),
                P("dp", "seq", None),
                P("dp", None),
            ),
            check_vma=False,
        )(queries, keys, values, out_weight, cotangent, block_mask)

    return program
```

```python
import math

import jax
import jax.numpy as jnp
from jax import lax
from jax.experimental import pallas as pl
from jax.experimental.pallas import tpu as pltpu
from jax.sharding import PartitionSpec as P

DH = 128
HALF = DH // 2
LOG2E = 1.4426950408889634
F32 = jnp.float32
BF16 = jnp.bfloat16
VMEM_BYTES = 56 * 1024 * 1024


SMEM = pl.BlockSpec(memory_space=pltpu.SMEM)
VMEM = pl.BlockSpec(memory_space=pltpu.VMEM)
HBM = pl.BlockSpec(memory_space=pl.ANY)


def call(kernel, name, operands, in_specs, out_shape, out_specs, scratch=(), flops=0, after=()):
    extra = len(after)

    def body(*refs):
        kernel(*refs[: len(operands)], *refs[len(operands) + extra :])

    nbytes = sum(x.size * x.dtype.itemsize for x in (*operands, *out_shape))
    return pl.pallas_call(
        body,
        in_specs=list(in_specs) + [HBM] * extra,
        out_specs=list(out_specs),
        out_shape=list(out_shape),
        scratch_shapes=list(scratch),
        compiler_params=pltpu.CompilerParams(vmem_limit_bytes=VMEM_BYTES),
        cost_estimate=pl.CostEstimate(flops=0, bytes_accessed=1024, transcendentals=0),
        name=name,
    )(*operands, *after)


def run_copies(pairs, sems, first=0):
    copies = [pltpu.make_async_copy(s, d, sems.at[first + i]) for i, (s, d) in enumerate(pairs)]
    for copy in copies:
        copy.start()
    return copies


def head_columns(place, column, head):
    at = 4 * jnp.bitwise_xor(place[2], head) + column
    return pl.ds(pl.multiple_of(at * DH, DH), DH)


def block_rows(place, flip, tokens):
    return pl.ds(pl.multiple_of(jnp.bitwise_xor(place[0], flip) * tokens, tokens), tokens)


def split_kernel(place, query, key, value, out):
    for column in range(4):
        for index, source in enumerate((query, key, value)):
            for h in range(4):
                out[column, index, :, h * DH : (h + 1) * DH] = source[:, head_columns(place, column, h)]


def split_heads(place, queries, keys, values, after=()):
    tokens, width = queries.shape
    out = jax.ShapeDtypeStruct((4, 3, tokens, width // 4), BF16)
    operands = (place, queries, keys, values)
    return call(split_kernel, "split_heads", operands, [SMEM] + [VMEM] * 3, [out], [VMEM], after=after)[0]


def chunk_kernel(place, own, got, chunk, part, sems):
    column, core = place[0], place[1]
    rows = pl.ds(pl.multiple_of((column % 2) * DH, DH), DH)
    owner = column // 2 == core
    pl.when(owner)(lambda: pltpu.make_async_copy(own.at[rows, :], chunk, sems.at[0]).start())
    pl.when(jnp.logical_not(owner))(lambda: pltpu.make_async_copy(got.at[rows, :], chunk, sems.at[0]).start())
    pltpu.make_async_copy(own.at[rows, :], chunk, sems.at[0]).wait()
    part[...] = chunk[pl.ds(pl.multiple_of(core * HALF, HALF), HALF), :]


def head_chunk(place, own, got, after=()):
    width = own.shape[1]
    out = [jax.ShapeDtypeStruct((rows, width), BF16) for rows in (DH, HALF)]
    scratch = [pltpu.SemaphoreType.DMA((1,))]
    return call(chunk_kernel, "head_chunk", (place, own, got), [SMEM, HBM, HBM], out, [VMEM] * 2, scratch, after=after)


def merge_kernel(place, blocks, *outs):
    for column in range(4):
        for index, target in enumerate(outs):
            for h in range(4):
                target[:, head_columns(place, column, h)] = blocks[column, index, :, h * DH : (h + 1) * DH]


def merge_heads(place, blocks, after=()):
    _, _, tokens, part = blocks.shape
    out = jax.ShapeDtypeStruct((tokens, 4 * part), BF16)
    return call(merge_kernel, "merge_heads", (place, blocks), [SMEM, VMEM], [out] * 3, [VMEM] * 3, after=after)


def dot(a, b, a_dim, b_dim):
    return lax.dot_general(a, b, (((a_dim,), (b_dim,)), ((), ())), preferred_element_type=F32)


def load_blocks(blocks, rows, sems, first):
    tokens = blocks.shape[2]
    return run_copies([(blocks.at[p], rows.at[:, pl.ds(p * tokens, tokens), :]) for p in range(4)], sems, first)


def load_cots(place, blocks, rows, sems, first):
    tokens = blocks[0].shape[0]
    pairs = [(b, rows.at[block_rows(place, p, tokens), :]) for p, b in enumerate(blocks[:3])]
    start = pl.multiple_of(jnp.bitwise_xor(place[0], 3) * tokens, tokens)
    for i, part in enumerate(blocks[3:]):
        pairs.append((part, rows.at[pl.ds(start + i * (tokens // 2), tokens // 2), :]))
    return run_copies(pairs, sems, first)


def load_slab(place, weights, slab, sems, first):
    own, direct, crossed, half, other_half = weights
    core = place[1]

    def rows(start, count):
        return slab.at[pl.ds(pl.multiple_of(start, HALF), count), :]

    pairs = [
        (own, rows(0, DH)),
        (direct, rows((1 + core) * DH, DH)),
        (crossed, rows((2 - core) * DH, DH)),
        (half, rows(3 * DH + core * HALF, HALF)),
        (other_half, rows(3 * DH + (1 - core) * HALF, HALF)),
    ]
    return run_copies(pairs, sems, first)


def bias_rows(mask):
    rows = []
    for r in range(4):
        row = []
        for p in range(4):
            kept = mask[p * 4 + r] > 0
            row.append(jnp.full((1, DH), jnp.where(kept, 0.0, -1e30), F32))
        rows.append(jnp.concatenate(row, axis=1))
    return rows


def scores_kq(bias, query, key):
    raw = dot(key, query, 1, 1) * (LOG2E / math.sqrt(DH))
    return jnp.concatenate([raw[r * DH : (r + 1) * DH] + bias[r] for r in range(4)], axis=0)


def forward_kernel(mask, blocks, attended, attended_t, log_total, qkv, sems):
    copies = load_blocks(blocks, qkv, sems, 0)
    bias = bias_rows(mask)
    for copy in copies:
        copy.wait()
    for h in range(4):
        here = slice(h * DH, (h + 1) * DH)
        scores = scores_kq(bias, qkv[0, :, here], qkv[1, :, here])
        highest = jnp.max(scores, axis=0, keepdims=True)
        weights = jnp.exp2(scores - highest)
        total = jnp.sum(weights, axis=0, keepdims=True)
        rounded = (weights * (1.0 / total)).astype(BF16)
        out_t = dot(qkv[2, :, here], rounded, 0, 0).astype(BF16)
        attended_t[here, :] = out_t
        attended[:, here] = out_t.T
        log_total[h : h + 1, :] = highest + jnp.log2(total)


def forward(mask, blocks, after=()):
    _, _, tokens, part = blocks.shape
    length = 4 * tokens
    return call(
        forward_kernel,
        "forward",
        (mask, blocks),
        [SMEM, HBM],
        [
            jax.ShapeDtypeStruct((length, part), BF16),
            jax.ShapeDtypeStruct((part, length), BF16),
            jax.ShapeDtypeStruct((4, length), F32),
        ],
        [VMEM] * 3,
        [pltpu.VMEM((3, length, part), BF16), pltpu.SemaphoreType.DMA((4,))],
        flops=4 * length * length * part,
        after=after,
    )


def mixed_kernel(place, w0, w1, w2, w3, w4, attended, send_x, send_y, own, x_right, y_left, slab, total, sems):
    copies = load_slab(place, (w0, w1, w2, w3, w4), slab, sems, 0)
    for copy in copies:
        copy.wait()
    tokens = attended.shape[0] // 4
    step = slab.shape[1] // 4
    for piece in range(4):
        columns = slice(piece * step, (piece + 1) * step)
        here = slice((piece % 2) * step, (piece % 2 + 1) * step)
        total[piece % 2] = dot(attended[...], slab[:, columns], 1, 0).astype(BF16)
        parts = [total.at[piece % 2][block_rows(place, flip, tokens), :] for flip in range(4)]
        own[:, columns] = parts[0]
        if piece < 2:
            send_x[0, :, here] = parts[1]
            send_x[1, :, here] = parts[3]
            y_left[:, here] = parts[2]
        else:
            send_y[0, :, here] = parts[2]
            send_y[1, :, here] = parts[3]
            x_right[:, here] = parts[1]


def mixed_parts(place, weights, attended, after=()):
    length, part = attended.shape
    width = weights[0].shape[1]
    tokens, half = length // 4, width // 2
    return call(
        mixed_kernel,
        "mixed_parts",
        (place, *weights, attended),
        [SMEM] + [HBM] * 5 + [VMEM],
        [
            jax.ShapeDtypeStruct((2, tokens, half), BF16),
            jax.ShapeDtypeStruct((2, tokens, half), BF16),
            jax.ShapeDtypeStruct((tokens, width), BF16),
            jax.ShapeDtypeStruct((tokens, half), BF16),
            jax.ShapeDtypeStruct((tokens, half), BF16),
        ],
        [VMEM] * 5,
        [
            pltpu.VMEM((part, width), BF16),
            pltpu.VMEM((2, length, width // 4), BF16),
            pltpu.SemaphoreType.DMA((5,)),
        ],
        flops=2 * length * width * part,
        after=after,
    )


def weight_kernel(place, attended_t, c0, c1, c2, c3, c4, keep, send, cots, sems):
    copies = load_cots(place, (c0, c1, c2, c3, c4), cots, sems, 0)
    core = place[1]
    rows = []
    for half in (1 - core, core):
        for h in range(4):
            rows.append(attended_t[pl.ds(pl.multiple_of(h * DH + half * HALF, HALF), HALF), :])
    left = jnp.concatenate(rows, axis=0)
    for copy in copies:
        copy.wait()
    step = cots.shape[1] // 4
    for piece in range(4):
        columns = slice(piece * step, (piece + 1) * step)
        total = dot(left, cots[:, columns], 1, 0).astype(BF16)
        for h in range(4):
            send[h, :, columns] = total[h * HALF : (h + 1) * HALF]
            keep[h, :, columns] = total[(4 + h) * HALF : (5 + h) * HALF]


def weight_parts(place, attended_t, cot_blocks, after=()):
    part, length = attended_t.shape
    width = cot_blocks[0].shape[1]
    out = jax.ShapeDtypeStruct((4, HALF, width), BF16)
    return call(
        weight_kernel,
        "weight_parts",
        (place, attended_t, *cot_blocks),
        [SMEM, VMEM] + [HBM] * 5,
        [out] * 2,
        [VMEM] * 2,
        [pltpu.VMEM((length, width), BF16), pltpu.SemaphoreType.DMA((5,))],
        flops=2 * length * width * part,
        after=after,
    )


def add_kernel(keep, got, *outs):
    for h, out in enumerate(outs):
        out[...] = (keep[h].astype(F32) + got[h].astype(F32)).astype(BF16)


def add_cores(keep, got, after=()):
    out = jax.ShapeDtypeStruct(keep.shape[1:], BF16)
    return call(add_kernel, "add_cores", (keep, got), [VMEM] * 2, [out] * 4, [VMEM] * 4, after=after)


def weight_out_kernel(place, p0, p1, p2, p3, out):
    for k, piece in enumerate((p0, p1, p2, p3)):
        head = jnp.bitwise_xor(place[0] % 2, k % 2)
        half = jnp.bitwise_xor(jnp.bitwise_xor(place[1], place[0] // 2), k // 2)
        start = pl.multiple_of(head * DH + half * HALF, HALF)
        out[pl.ds(start, HALF), :] = piece[...].astype(F32) * 0.125


def weight_out(place, pieces):
    rows, width = pieces[0].shape
    out = jax.ShapeDtypeStruct((4 * rows, width), F32)
    return call(weight_out_kernel, "weight_out", (place, *pieces), [SMEM] + [VMEM] * 4, [out], [VMEM])[0]


def grads_kernel(place, w0, w1, w2, w3, w4, c0, c1, c2, c3, c4, grads, slab, cots, sems):
    copies = load_slab(place, (w0, w1, w2, w3, w4), slab, sems, 0)
    copies += load_cots(place, (c0, c1, c2, c3, c4), cots, sems, 5)
    for copy in copies:
        copy.wait()
    for pair in range(2):
        rows = slice(pair * 2 * DH, (pair + 1) * 2 * DH)
        grads[:, rows] = dot(cots[...], slab[rows, :], 1, 1).astype(BF16)


def attended_grads(place, weights, cot_blocks, after=()):
    tokens, width = cot_blocks[0].shape
    part, length = 4 * DH, 4 * tokens
    return call(
        grads_kernel,
        "attended_grads",
        (place, *weights, *cot_blocks),
        [SMEM] + [HBM] * 10,
        [jax.ShapeDtypeStruct((length, part), BF16)],
        [VMEM],
        [pltpu.VMEM((part, width), BF16), pltpu.VMEM((length, width), BF16), pltpu.SemaphoreType.DMA((10,))],
        flops=2 * length * width * part,
        after=after,
    )[0]


def backward_kernel(mask, log_total, grads, blocks, out, qkv, sems):
    copies = load_blocks(blocks, qkv, sems, 0)
    tokens = out.shape[2]
    scale = 1.0 / math.sqrt(DH)
    bias = bias_rows(mask)
    for copy in copies:
        copy.wait()
    for h in range(4):
        here = slice(h * DH, (h + 1) * DH)
        query, key, value, grad = qkv[0, :, here], qkv[1, :, here], qkv[2, :, here], grads[:, here]
        probs = jnp.exp2(scores_kq(bias, query, key) - log_total[h : h + 1, :])
        grad_value = dot(probs.astype(BF16), grad, 1, 0).astype(BF16)
        grad_probs = dot(value, grad, 1, 1)
        delta = jnp.sum(probs * grad_probs, axis=0, keepdims=True)
        grad_scores = (probs * (grad_probs - delta) * scale).astype(BF16)
        grad_key = dot(grad_scores, query, 1, 0).astype(BF16)
        grad_query = dot(key, grad_scores, 0, 0).astype(BF16).T
        for index, full in enumerate((grad_query, grad_key, grad_value)):
            for p in range(4):
                out[p, index, :, here] = full[p * tokens : (p + 1) * tokens]


def backward(mask, log_total, grads, blocks, after=()):
    _, _, tokens, part = blocks.shape
    length = 4 * tokens
    return call(
        backward_kernel,
        "backward",
        (mask, log_total, grads, blocks),
        [SMEM] + [VMEM] * 2 + [HBM],
        [jax.ShapeDtypeStruct(blocks.shape, BF16)],
        [VMEM],
        [pltpu.VMEM((3, length, part), BF16), pltpu.SemaphoreType.DMA((4,))],
        flops=10 * length * length * part,
        after=after,
    )[0]


def column_shards(queries, keys, values, out_weight, cotangent, block_mask):
    tokens, width = queries.shape[1:]
    column = lax.axis_index("seq")
    rank = lax.axis_index("dp")
    core, z = rank % 2, rank // 2
    place = jnp.stack([column, core, z]).astype(jnp.int32)
    mask = block_mask.reshape(-1)
    cot = cotangent[0]

    def plane(array, flip):
        return lax.ppermute(array, "seq", [(i, i ^ flip) for i in range(4)])

    def swap(array):
        return lax.ppermute(array, "dp", [(i, i ^ 1) for i in range(8)])

    def along(array, flip):
        return lax.ppermute(array, "dp", [(i, i ^ (2 * flip)) for i in range(8)])

    def columns(array):
        return lax.all_to_all(array, "seq", 0, 0, tiled=True)

    heads = split_heads(place, queries[0], keys[0], values[0])
    blocks = columns(heads)

    cot_x, cot_y = plane(cot, 1), plane(cot, 2)

    def in_dp(array, target):
        return lax.ppermute(array, "dp", [(2 * a + c, target(a, c)) for a in range(4) for c in range(2)])

    chunk, part = head_chunk(place, out_weight, swap(out_weight), after=(heads,))
    direct = in_dp(chunk, lambda a, c: 2 * (a ^ (1 + c)) + c)
    part = in_dp(part, lambda a, c: 2 * (a ^ 3) + c)

    attended, attended_t, log_total = forward(mask, blocks)

    cot_x, cot_y, direct, part, attended = lax.optimization_barrier((cot_x, cot_y, direct, part, attended))
    half = tokens // 2
    cot_blocks = (cot, cot_x, cot_y, plane(cot_y[:half], 1), plane(cot_x[half:], 2))
    weights = (chunk, direct, swap(direct), part, swap(part))

    send_x, send_y, mixed_own, x_right, y_left = mixed_parts(place, weights, attended)
    got_x, got_y = plane(send_x, 1), plane(send_y, 2)
    got_left = plane((y_left.astype(F32) + got_x[1].astype(F32)).astype(BF16), 2)
    got_right = plane((x_right.astype(F32) + got_y[1].astype(F32)).astype(BF16), 1)
    mixed = jnp.concatenate(
        [
            mixed_own[:, : width // 2].astype(F32) + got_x[0].astype(F32) + got_left.astype(F32),
            mixed_own[:, width // 2 :].astype(F32) + got_y[0].astype(F32) + got_right.astype(F32),
        ],
        axis=1,
    ).astype(BF16)

    keep, send = weight_parts(place, attended_t, cot_blocks, after=(send_x,))
    grads = attended_grads(place, weights, cot_blocks, after=(keep,))
    s0, s1, s2, s3 = add_cores(keep, swap(send), after=(grads,))
    got = [along(s, flip).astype(F32) for flip, s in ((1, s1), (2, s2), (3, s3))]
    summed = (s0.astype(F32) + got[0] + got[1] + got[2]).astype(BF16)
    pieces = []
    for k in range(4):
        pairs = []
        for plane_at in range(4):
            for c in range(2):
                for t in range(4):
                    to_core, to_column = t // 2, t ^ (2 * c) ^ k
                    pairs.append(((2 * plane_at + c) * 4 + t, (2 * plane_at + to_core) * 4 + to_column))
        pieces.append(lax.ppermute(summed, ("dp", "seq"), pairs))
    grad_weight = weight_out(place, pieces)

    outs = columns(backward(mask, log_total, grads, blocks, after=(s1,)))
    merged = merge_heads(place, outs, after=(summed,))
    return (mixed[None],) + tuple(g[None] for g in merged) + (grad_weight,)


def attend(query_heads, key_heads, value_heads, grad_heads, block_mask):
    batch, length, width = query_heads.shape
    heads = width // DH
    shape_split = (batch, length, heads, DH)
    query_split = query_heads.reshape(shape_split)
    key_split = key_heads.reshape(shape_split)
    value_split = value_heads.reshape(shape_split)
    grad_split = grad_heads.reshape(shape_split)
    block = length // block_mask.shape[2]
    rows_step = min(512, length)
    scale = 1.0 / math.sqrt(DH)

    def step(carry, index):
        key_total, value_total = carry
        start = index * rows_step
        query_part = lax.dynamic_slice_in_dim(query_split, start, rows_step, 1)
        grad_part = lax.dynamic_slice_in_dim(grad_split, start, rows_step, 1)
        mask_part = lax.dynamic_slice_in_dim(block_mask, start // block, rows_step // block, 1)
        allowed = jnp.repeat(jnp.repeat(mask_part, block, axis=1), block, axis=2) > 0
        scores = (
            jnp.einsum("bqhd,bkhd->bhqk", query_part, key_split, preferred_element_type=jnp.float32)
            * scale
        )
        scores = jnp.where(allowed[:, None], scores, -1e30)
        highest = jnp.max(scores, axis=3, keepdims=True)
        log_total = highest + jnp.log(jnp.sum(jnp.exp(scores - highest), axis=3, keepdims=True))
        probs = jnp.exp(scores - log_total)
        rounded = probs.astype(jnp.bfloat16)
        attended = jnp.einsum(
            "bhqk,bkhd->bqhd", rounded, value_split, preferred_element_type=jnp.float32
        ).astype(jnp.bfloat16)
        value_total = value_total + jnp.einsum(
            "bhqk,bqhd->bkhd", rounded, grad_part, preferred_element_type=jnp.float32
        )
        grad_probs = jnp.einsum(
            "bqhd,bkhd->bhqk", grad_part, value_split, preferred_element_type=jnp.float32
        )
        delta = jnp.sum(probs * grad_probs, axis=3, keepdims=True)
        grad_scores = (probs * (grad_probs - delta) * scale).astype(jnp.bfloat16)
        grad_query = jnp.einsum(
            "bhqk,bkhd->bqhd", grad_scores, key_split, preferred_element_type=jnp.float32
        ).astype(jnp.bfloat16)
        key_total = key_total + jnp.einsum(
            "bhqk,bqhd->bkhd", grad_scores, query_part, preferred_element_type=jnp.float32
        )
        return ((key_total, value_total), (attended, grad_query))

    zeros = jnp.zeros(shape_split, jnp.float32)
    totals, pieces = lax.scan(
        step, (zeros, zeros), jnp.arange(length // rows_step, dtype=jnp.int32)
    )

    def joined(parts):
        return jnp.moveaxis(parts, 0, 1).reshape(batch, length, width)

    grad_key = totals[0].astype(jnp.bfloat16).reshape(batch, length, width)
    grad_value = totals[1].astype(jnp.bfloat16).reshape(batch, length, width)
    return (joined(pieces[0]), joined(pieces[1]), grad_key, grad_value)


def general_shards(queries, keys, values, out_weight, cotangent, block_mask):
    batch, tokens, width = queries.shape
    query_heads, key_heads, value_heads = (
        lax.all_to_all(queries, "seq", split_axis=2, concat_axis=1, tiled=True),
        lax.all_to_all(keys, "seq", split_axis=2, concat_axis=1, tiled=True),
        lax.all_to_all(values, "seq", split_axis=2, concat_axis=1, tiled=True),
    )
    weight_full = lax.all_gather(out_weight, "dp", axis=0, tiled=True)
    flat_cot = cotangent.reshape(batch * tokens, width)
    grad_attn = lax.dot_general(
        flat_cot, weight_full, (((1,), (1,)), ((), ())), preferred_element_type=jnp.float32
    )
    grad_attn = grad_attn.astype(jnp.bfloat16).reshape(batch, tokens, width)
    grad_heads = lax.all_to_all(grad_attn, "seq", split_axis=2, concat_axis=1, tiled=True)
    attended_heads, grad_q_heads, grad_k_heads, grad_v_heads = attend(
        query_heads, key_heads, value_heads, grad_heads, block_mask
    )
    attended, grad_queries, grad_keys, grad_values = (
        lax.all_to_all(attended_heads, "seq", split_axis=1, concat_axis=2, tiled=True),
        lax.all_to_all(grad_q_heads, "seq", split_axis=1, concat_axis=2, tiled=True),
        lax.all_to_all(grad_k_heads, "seq", split_axis=1, concat_axis=2, tiled=True),
        lax.all_to_all(grad_v_heads, "seq", split_axis=1, concat_axis=2, tiled=True),
    )
    flat_att = attended.reshape(batch * tokens, width)
    mixed = (
        jnp.dot(flat_att, weight_full, preferred_element_type=jnp.float32)
        .astype(jnp.bfloat16)
        .reshape(batch, tokens, width)
    )
    partial_grad = lax.psum_scatter(
        lax.dot_general(
            flat_att, flat_cot, (((0,), (0,)), ((), ())), preferred_element_type=jnp.float32
        ),
        "dp",
        scatter_dimension=0,
        tiled=True,
    )
    summed = lax.psum(partial_grad, "seq")
    grad_weight = summed / (batch * lax.axis_size("dp"))
    return (mixed, grad_queries, grad_keys, grad_values, grad_weight)


def fits_columns(mesh, queries, out_weight, block_mask):
    batch, length, width = queries
    return (
        mesh.shape["dp"] == 8
        and mesh.shape["seq"] == 4
        and batch == 8
        and length == 4 * DH
        and width == 16 * DH
        and out_weight == (width, width)
        and block_mask == (batch, 4, 4)
    )


def solution(mesh):
    placed = (
        P("dp", "seq", None),
        P("dp", "seq", None),
        P("dp", "seq", None),
        P("dp", None),
        P("dp", "seq", None),
        P("dp", None, None),
    )

    def program(queries, keys, values, out_weight, cotangent, block_mask):
        fits = fits_columns(mesh, queries.shape, out_weight.shape, block_mask.shape)
        return jax.shard_map(
            column_shards if fits else general_shards,
            mesh=mesh,
            in_specs=placed,
            out_specs=(
                P("dp", "seq", None),
                P("dp", "seq", None),
                P("dp", "seq", None),
                P("dp", "seq", None),
                P("dp", None),
            ),
            check_vma=False,
        )(queries, keys, values, out_weight, cotangent, block_mask)

    return program
```

```python
import math

import jax
import jax.numpy as jnp
from jax import lax
from jax.experimental import pallas as pl
from jax.experimental.pallas import tpu as pltpu
from jax.sharding import PartitionSpec as P

DH = 128
HALF = DH // 2
LOG2E = 1.4426950408889634
F32 = jnp.float32
BF16 = jnp.bfloat16
VMEM_BYTES = 20 * 1024 * 1024
HINT = 8_000_000_000


SMEM = pl.BlockSpec(memory_space=pltpu.SMEM)
VMEM = pl.BlockSpec(memory_space=pltpu.VMEM)
HBM = pl.BlockSpec(memory_space=pl.ANY)
FAR = pl.BlockSpec(memory_space=pltpu.HBM)


def call(kernel, name, operands, in_specs, out_shape, out_specs, scratch=(), hint=0, after=(), vmem=VMEM_BYTES):
    extra = len(after)

    def body(*refs):
        kernel(*refs[: len(operands)], *refs[len(operands) + extra :])

    return pl.pallas_call(
        body,
        in_specs=list(in_specs) + [HBM] * extra,
        out_specs=list(out_specs),
        out_shape=list(out_shape),
        scratch_shapes=list(scratch),
        compiler_params=pltpu.CompilerParams(vmem_limit_bytes=vmem),
        cost_estimate=pl.CostEstimate(flops=hint, bytes_accessed=1024, transcendentals=0),
        name=name,
    )(*operands, *after)


def run_copies(pairs, sems, first=0):
    copies = [pltpu.make_async_copy(s, d, sems.at[first + i]) for i, (s, d) in enumerate(pairs)]
    for copy in copies:
        copy.start()
    return copies


def head_columns(place, column, head):
    at = 4 * jnp.bitwise_xor(place[2], head) + column
    return pl.ds(pl.multiple_of(at * DH, DH), DH)


def block_rows(place, flip, tokens):
    return pl.ds(pl.multiple_of(jnp.bitwise_xor(place[0], flip) * tokens, tokens), tokens)


def split_kernel(place, query, key, value, out, held, sems):
    loads = run_copies([(source, held.at[index]) for index, source in enumerate((query, key, value))], sems)
    for index in range(3):
        loads[index].wait()
        for column in range(4):
            for h in range(4):
                out[column, index, :, h * DH : (h + 1) * DH] = held[index, :, head_columns(place, column, h)]


def split_heads(place, queries, keys, values, after=()):
    tokens, width = queries.shape
    out = jax.ShapeDtypeStruct((4, 3, tokens, width // 4), BF16)
    operands = (place, queries, keys, values)
    scratch = [pltpu.VMEM((3, tokens, width), BF16), pltpu.SemaphoreType.DMA((3,))]
    return call(split_kernel, "split_heads", operands, [SMEM] + [FAR] * 3, [out], [VMEM], scratch, after=after, vmem=3 * VMEM_BYTES)[0]


def chunk_kernel(place, own, got, chunk, part, sems):
    column, core = place[0], place[1]
    rows = pl.ds(pl.multiple_of((column % 2) * DH, DH), DH)
    owner = column // 2 == core
    pl.when(owner)(lambda: pltpu.make_async_copy(own.at[rows, :], chunk, sems.at[0]).start())
    pl.when(jnp.logical_not(owner))(lambda: pltpu.make_async_copy(got.at[rows, :], chunk, sems.at[0]).start())
    pltpu.make_async_copy(own.at[rows, :], chunk, sems.at[0]).wait()
    part[...] = chunk[pl.ds(pl.multiple_of(core * HALF, HALF), HALF), :]


def head_chunk(place, own, got, after=()):
    width = own.shape[1]
    out = [jax.ShapeDtypeStruct((rows, width), BF16) for rows in (DH, HALF)]
    scratch = [pltpu.SemaphoreType.DMA((1,))]
    return call(chunk_kernel, "head_chunk", (place, own, got), [SMEM, FAR, HBM], out, [VMEM] * 2, scratch, after=after)


def merge_kernel(place, blocks, *outs):
    for column in range(4):
        for index, target in enumerate(outs):
            for h in range(4):
                target[:, head_columns(place, column, h)] = blocks[column, index, :, h * DH : (h + 1) * DH]


def merge_heads(place, blocks, after=()):
    _, _, tokens, part = blocks.shape
    out = jax.ShapeDtypeStruct((tokens, 4 * part), BF16)
    return call(merge_kernel, "merge_heads", (place, blocks), [SMEM, VMEM], [out] * 3, [VMEM] * 3, after=after)


def dot(a, b, a_dim, b_dim):
    return lax.dot_general(a, b, (((a_dim,), (b_dim,)), ((), ())), preferred_element_type=F32)


def head_lanes(h):
    return pl.ds(h * DH, DH)


def load_heads(blocks, rows, sems):
    tokens = blocks.shape[2]
    return run_copies([(blocks.at[p], rows.at[:, pl.ds(p * tokens, tokens), :]) for p in range(4)], sems)


def load_pieces(pairs, sems, first, count):
    step = pairs[0][0].shape[1] // count
    copies = []
    for i in range(count):
        columns = pl.ds(i * step, step)
        copies.append(run_copies([(s.at[:, columns], d(columns)) for s, d in pairs], sems, first + i * len(pairs)))
    return copies


def cot_pairs(place, blocks, rows):
    tokens = blocks[0].shape[0]

    def target(flip, offset, count):
        start = pl.multiple_of(jnp.bitwise_xor(place[0], flip) * tokens + offset, HALF)
        return lambda columns: rows.at[pl.ds(start, count), columns]

    pairs = [(b, target(p, 0, tokens)) for p, b in enumerate(blocks[:3])]
    return pairs + [(b, target(3, i * (tokens // 2), tokens // 2)) for i, b in enumerate(blocks[3:])]


def slab_pairs(place, weights, slab):
    own, direct, crossed, half, other_half = weights
    core = place[1]

    def target(start, count):
        return lambda columns: slab.at[pl.ds(pl.multiple_of(start, HALF), count), columns]

    return [
        (own, target(0, DH)),
        (direct, target((1 + core) * DH, DH)),
        (crossed, target((2 - core) * DH, DH)),
        (half, target(3 * DH + core * HALF, HALF)),
        (other_half, target(3 * DH + (1 - core) * HALF, HALF)),
    ]


def wait_all(copies):
    for copy in copies:
        copy.wait()


def bias_rows(mask):
    rows = []
    for r in range(4):
        row = []
        for p in range(4):
            kept = mask[p * 4 + r] > 0
            row.append(jnp.full((1, DH), jnp.where(kept, 0.0, -1e30), F32))
        rows.append(jnp.concatenate(row, axis=1))
    return rows


def scores_kq(bias, query, key):
    raw = dot(key, query, 1, 1) * (LOG2E / math.sqrt(DH))
    return jnp.concatenate([raw[r * DH : (r + 1) * DH] + bias[r] for r in range(4)], axis=0)


def forward_kernel(mask, blocks, attended, attended_t, log_total, qkv, sems):
    copies = load_heads(blocks, qkv, sems)
    bias = bias_rows(mask)
    wait_all(copies)
    for h in range(4):
        here = slice(h * DH, (h + 1) * DH)
        scores = scores_kq(bias, qkv[0, :, here], qkv[1, :, here])
        highest = jnp.max(scores, axis=0, keepdims=True)
        weights = jnp.exp2(scores - highest)
        total = jnp.sum(weights, axis=0, keepdims=True)
        rounded = (weights * (1.0 / total)).astype(BF16)
        out_t = dot(qkv[2, :, here], rounded, 0, 0).astype(BF16)
        attended_t[here, :] = out_t
        attended[:, here] = out_t.T
        log_total[h : h + 1, :] = highest + jnp.log2(total)


def forward(mask, blocks, after=()):
    _, _, tokens, part = blocks.shape
    length = 4 * tokens
    return call(
        forward_kernel,
        "forward",
        (mask, blocks),
        [SMEM, HBM],
        [
            jax.ShapeDtypeStruct((length, part), BF16),
            jax.ShapeDtypeStruct((part, length), BF16),
            jax.ShapeDtypeStruct((4, length), F32),
        ],
        [VMEM] * 3,
        [pltpu.VMEM((3, length, part), BF16), pltpu.SemaphoreType.DMA((4,))],
        after=after,
    )


def mixed_kernel(place, w0, w1, w2, w3, w4, attended, send_x, send_y, own, x_right, y_left, slab, total, sems):
    wait_all(load_pieces(slab_pairs(place, (w0, w1, w2, w3, w4), slab), sems, 0, 1)[0])
    tokens = attended.shape[0] // 4
    step = slab.shape[1] // 4
    for piece in range(4):
        columns = slice(piece * step, (piece + 1) * step)
        here = slice((piece % 2) * step, (piece % 2 + 1) * step)
        total[piece % 2] = dot(attended[...], slab[:, columns], 1, 0).astype(BF16)
        parts = [total.at[piece % 2][block_rows(place, flip, tokens), :] for flip in range(4)]
        own[:, columns] = parts[0]
        if piece < 2:
            send_x[0, :, here] = parts[1]
            send_x[1, :, here] = parts[3]
            y_left[:, here] = parts[2]
        else:
            send_y[0, :, here] = parts[2]
            send_y[1, :, here] = parts[3]
            x_right[:, here] = parts[1]


def mixed_parts(place, weights, attended, after=()):
    length, part = attended.shape
    width = weights[0].shape[1]
    tokens, half = length // 4, width // 2
    return call(
        mixed_kernel,
        "mixed_parts",
        (place, *weights, attended),
        [SMEM] + [HBM] * 5 + [VMEM],
        [
            jax.ShapeDtypeStruct((2, tokens, half), BF16),
            jax.ShapeDtypeStruct((2, tokens, half), BF16),
            jax.ShapeDtypeStruct((tokens, width), BF16),
            jax.ShapeDtypeStruct((tokens, half), BF16),
            jax.ShapeDtypeStruct((tokens, half), BF16),
        ],
        [VMEM] * 5,
        [
            pltpu.VMEM((part, width), BF16),
            pltpu.VMEM((2, length, width // 4), BF16),
            pltpu.SemaphoreType.DMA((5,)),
        ],
        after=after,
    )


def second_kernel(x_right, y_left, got_x, got_y, left, right):
    left[...] = (y_left[...].astype(F32) + got_x[1].astype(F32)).astype(BF16)
    right[...] = (x_right[...].astype(F32) + got_y[1].astype(F32)).astype(BF16)


def second_parts(x_right, y_left, got_x, got_y, after=()):
    out = jax.ShapeDtypeStruct(x_right.shape, BF16)
    operands = (x_right, y_left, got_x, got_y)
    return call(second_kernel, "second_parts", operands, [VMEM] * 4, [out] * 2, [VMEM] * 2, hint=HINT, after=after)


def weight_kernel(place, attended_t, c0, c1, c2, c3, c4, keep, send, cots, kept, sent, sems):
    loads = load_pieces(cot_pairs(place, (c0, c1, c2, c3, c4), cots), sems, 0, 1)[0]
    core = place[1]
    rows = []
    for half in (1 - core, core):
        for h in range(4):
            rows.append(attended_t[pl.ds(pl.multiple_of(h * DH + half * HALF, HALF), HALF), :])
    left = jnp.concatenate(rows, axis=0)
    step = cots.shape[1] // 4
    stores = []
    wait_all(loads)
    for piece in range(4):
        columns = slice(piece * step, (piece + 1) * step)
        total = dot(left, cots[:, columns], 1, 0).astype(BF16)
        for h in range(4):
            sent[h, :, columns] = total[h * HALF : (h + 1) * HALF]
            kept[h, :, columns] = total[(4 + h) * HALF : (5 + h) * HALF]
        window = pl.ds(piece * step, step)
        pairs = [(sent.at[:, :, window], send.at[:, :, window]), (kept.at[:, :, window], keep.at[:, :, window])]
        stores += run_copies(pairs, sems, 5 + 2 * piece)
    wait_all(stores)


def weight_parts(place, attended_t, cot_blocks, after=()):
    part, length = attended_t.shape
    width = cot_blocks[0].shape[1]
    out = jax.ShapeDtypeStruct((4, HALF, width), BF16)
    return call(
        weight_kernel,
        "weight_parts",
        (place, attended_t, *cot_blocks),
        [SMEM, VMEM] + [HBM] * 5,
        [out] * 2,
        [HBM] * 2,
        [
            pltpu.VMEM((length, width), BF16),
            pltpu.VMEM((4, HALF, width), BF16),
            pltpu.VMEM((4, HALF, width), BF16),
            pltpu.SemaphoreType.DMA((13,)),
        ],
        after=after,
    )


def add_kernel(keep, got, *outs):
    for h, out in enumerate(outs):
        out[...] = (keep[h].astype(F32) + got[h].astype(F32)).astype(BF16)


def add_cores(keep, got, after=()):
    out = jax.ShapeDtypeStruct(keep.shape[1:], BF16)
    return call(add_kernel, "add_cores", (keep, got), [VMEM] * 2, [out] * 4, [VMEM] * 4, after=after)


def sum_kernel(p0, p1, p2, p3, out):
    out[...] = (p0[...].astype(F32) + p1[...].astype(F32) + p2[...].astype(F32) + p3[...].astype(F32)).astype(BF16)


def sum_planes(*parts):
    out = jax.ShapeDtypeStruct(parts[0].shape, BF16)
    return call(sum_kernel, "sum_planes", parts, [VMEM] * 4, [out], [VMEM], hint=0)[0]


def weight_out_kernel(place, p0, p1, p2, p3, out):
    for k, piece in enumerate((p0, p1, p2, p3)):
        head = jnp.bitwise_xor(place[0] % 2, k % 2)
        half = jnp.bitwise_xor(jnp.bitwise_xor(place[1], place[0] // 2), k // 2)
        start = pl.multiple_of(head * DH + half * HALF, HALF)
        out[pl.ds(start, HALF), :] = piece[...].astype(F32) * 0.125


def weight_out(place, pieces, after=()):
    rows, width = pieces[0].shape
    out = jax.ShapeDtypeStruct((4 * rows, width), F32)
    return call(weight_out_kernel, "weight_out", (place, *pieces), [SMEM] + [VMEM] * 4, [out], [VMEM], after=after)[0]


def grads_kernel(place, w0, w1, w2, w3, w4, c0, c1, c2, c3, c4, grads, slab, cots, sems):
    loads = load_pieces(slab_pairs(place, (w0, w1, w2, w3, w4), slab), sems, 0, 1)
    loads += load_pieces(cot_pairs(place, (c0, c1, c2, c3, c4), cots), sems, 5, 1)
    wait_all(loads[0] + loads[1])
    for pair in range(2):
        rows = slice(pair * 2 * DH, (pair + 1) * 2 * DH)
        grads[:, rows] = dot(cots[...], slab[rows, :], 1, 1).astype(BF16)


def attended_grads(place, weights, cot_blocks, after=()):
    tokens, width = cot_blocks[0].shape
    part, length = 4 * DH, 4 * tokens
    return call(
        grads_kernel,
        "attended_grads",
        (place, *weights, *cot_blocks),
        [SMEM] + [HBM] * 10,
        [jax.ShapeDtypeStruct((length, part), BF16)],
        [VMEM],
        [
            pltpu.VMEM((part, width), BF16),
            pltpu.VMEM((length, width), BF16),
            pltpu.SemaphoreType.DMA((10,)),
        ],
        after=after,
    )[0]


def backward_kernel(mask, log_total, grads, blocks, out, qkv, made, sems):
    loads = load_heads(blocks, qkv, sems)
    tokens = out.shape[2]
    scale = 1.0 / math.sqrt(DH)
    bias = bias_rows(mask)
    stores = []
    wait_all(loads)
    for h in range(4):
        here = slice(h * DH, (h + 1) * DH)
        query, key, value, grad = qkv[0, :, here], qkv[1, :, here], qkv[2, :, here], grads[:, here]
        probs = jnp.exp2(scores_kq(bias, query, key) - log_total[h : h + 1, :])
        grad_value = dot(probs.astype(BF16), grad, 1, 0).astype(BF16)
        grad_probs = dot(value, grad, 1, 1)
        delta = jnp.sum(probs * grad_probs, axis=0, keepdims=True)
        grad_scores = (probs * (grad_probs - delta) * scale).astype(BF16)
        grad_key = dot(grad_scores, query, 1, 0).astype(BF16)
        grad_query = dot(key, grad_scores, 0, 0).astype(BF16).T
        for index, full in enumerate((grad_query, grad_key, grad_value)):
            for p in range(4):
                made[p, index, :, here] = full[p * tokens : (p + 1) * tokens]
        stores += run_copies([(made.at[:, :, :, head_lanes(h)], out.at[:, :, :, head_lanes(h)])], sems, 4 + h)
    wait_all(stores)


def backward(mask, log_total, grads, blocks, after=()):
    _, _, tokens, part = blocks.shape
    length = 4 * tokens
    return call(
        backward_kernel,
        "backward",
        (mask, log_total, grads, blocks),
        [SMEM] + [VMEM] * 2 + [HBM],
        [jax.ShapeDtypeStruct(blocks.shape, BF16)],
        [HBM],
        [pltpu.VMEM((3, length, part), BF16), pltpu.VMEM(blocks.shape, BF16), pltpu.SemaphoreType.DMA((8,))],
        after=after,
    )[0]


def column_shards(queries, keys, values, out_weight, cotangent, block_mask):
    tokens, width = queries.shape[1:]
    column = lax.axis_index("seq")
    rank = lax.axis_index("dp")
    core, z = rank % 2, rank // 2
    place = jnp.stack([column, core, z]).astype(jnp.int32)
    mask = block_mask.reshape(-1)
    cot = cotangent[0]

    def plane(array, flip):
        return lax.ppermute(array, "seq", [(i, i ^ flip) for i in range(4)])

    def swap(array):
        return lax.ppermute(array, "dp", [(i, i ^ 1) for i in range(8)])

    def along(array, flip):
        return lax.ppermute(array, "dp", [(i, i ^ (2 * flip)) for i in range(8)])

    def columns(array):
        return lax.all_to_all(array, "seq", 0, 0, tiled=True)

    heads = split_heads(place, queries[0], keys[0], values[0])
    blocks = columns(heads)

    cot_x, cot_y = plane(cot, 1), plane(cot, 2)

    def in_dp(array, target):
        return lax.ppermute(array, "dp", [(2 * a + c, target(a, c)) for a in range(4) for c in range(2)])

    chunk, part = head_chunk(place, out_weight, swap(out_weight), after=(heads,))
    direct = in_dp(chunk, lambda a, c: 2 * (a ^ (1 + c)) + c)
    part = in_dp(part, lambda a, c: 2 * (a ^ 3) + c)

    attended, attended_t, log_total = forward(mask, blocks)

    direct, part, attended = lax.optimization_barrier((direct, part, attended))
    weights = (chunk, direct, swap(direct), part, swap(part))

    send_x, send_y, mixed_own, x_right, y_left = mixed_parts(place, weights, attended)
    got_x, got_y = plane(send_x, 1), plane(send_y, 2)
    cot_x, cot_y, attended_t = lax.optimization_barrier((cot_x, cot_y, attended_t))
    half = tokens // 2
    cot_blocks = (cot, cot_x, cot_y, plane(cot_y[:half], 1), plane(cot_x[half:], 2))

    keep, send = weight_parts(place, attended_t, cot_blocks, after=(send_x,))
    grads = attended_grads(place, weights, cot_blocks, after=(keep,))
    s0, s1, s2, s3 = add_cores(keep, swap(send), after=(grads,))
    got = [along(s, flip).astype(F32) for flip, s in ((1, s1), (2, s2), (3, s3))]
    summed = (s0.astype(F32) + got[0] + got[1] + got[2]).astype(BF16)
    left, right = second_parts(x_right, y_left, got_x, got_y, after=(s1,))
    got_left, got_right = plane(left, 2), plane(right, 1)
    outs = columns(backward(mask, log_total, grads, blocks, after=(left,)))
    mixed = jnp.concatenate(
        [
            mixed_own[:, : width // 2].astype(F32) + got_x[0].astype(F32) + got_left.astype(F32),
            mixed_own[:, width // 2 :].astype(F32) + got_y[0].astype(F32) + got_right.astype(F32),
        ],
        axis=1,
    ).astype(BF16)

    pieces = []
    for k in range(4):
        pairs = []
        for plane_at in range(4):
            for c in range(2):
                for t in range(4):
                    to_core, to_column = t // 2, t ^ (2 * c) ^ k
                    pairs.append(((2 * plane_at + c) * 4 + t, (2 * plane_at + to_core) * 4 + to_column))
        pieces.append(lax.ppermute(summed, ("dp", "seq"), pairs))
    merged = merge_heads(place, outs, after=(summed, mixed))
    grad_weight = weight_out(place, pieces, after=(merged[0],))
    return (mixed[None],) + tuple(g[None] for g in merged) + (grad_weight,)


def attend(query_heads, key_heads, value_heads, grad_heads, block_mask):
    batch, length, width = query_heads.shape
    heads = width // DH
    shape_split = (batch, length, heads, DH)
    query_split = query_heads.reshape(shape_split)
    key_split = key_heads.reshape(shape_split)
    value_split = value_heads.reshape(shape_split)
    grad_split = grad_heads.reshape(shape_split)
    block = length // block_mask.shape[2]
    rows_step = min(512, length)
    scale = 1.0 / math.sqrt(DH)

    def step(carry, index):
        key_total, value_total = carry
        start = index * rows_step
        query_part = lax.dynamic_slice_in_dim(query_split, start, rows_step, 1)
        grad_part = lax.dynamic_slice_in_dim(grad_split, start, rows_step, 1)
        mask_part = lax.dynamic_slice_in_dim(block_mask, start // block, rows_step // block, 1)
        allowed = jnp.repeat(jnp.repeat(mask_part, block, axis=1), block, axis=2) > 0
        scores = (
            jnp.einsum("bqhd,bkhd->bhqk", query_part, key_split, preferred_element_type=jnp.float32)
            * scale
        )
        scores = jnp.where(allowed[:, None], scores, -1e30)
        highest = jnp.max(scores, axis=3, keepdims=True)
        log_total = highest + jnp.log(jnp.sum(jnp.exp(scores - highest), axis=3, keepdims=True))
        probs = jnp.exp(scores - log_total)
        rounded = probs.astype(jnp.bfloat16)
        attended = jnp.einsum(
            "bhqk,bkhd->bqhd", rounded, value_split, preferred_element_type=jnp.float32
        ).astype(jnp.bfloat16)
        value_total = value_total + jnp.einsum(
            "bhqk,bqhd->bkhd", rounded, grad_part, preferred_element_type=jnp.float32
        )
        grad_probs = jnp.einsum(
            "bqhd,bkhd->bhqk", grad_part, value_split, preferred_element_type=jnp.float32
        )
        delta = jnp.sum(probs * grad_probs, axis=3, keepdims=True)
        grad_scores = (probs * (grad_probs - delta) * scale).astype(jnp.bfloat16)
        grad_query = jnp.einsum(
            "bhqk,bkhd->bqhd", grad_scores, key_split, preferred_element_type=jnp.float32
        ).astype(jnp.bfloat16)
        key_total = key_total + jnp.einsum(
            "bhqk,bqhd->bkhd", grad_scores, query_part, preferred_element_type=jnp.float32
        )
        return ((key_total, value_total), (attended, grad_query))

    zeros = jnp.zeros(shape_split, jnp.float32)
    totals, pieces = lax.scan(
        step, (zeros, zeros), jnp.arange(length // rows_step, dtype=jnp.int32)
    )

    def joined(parts):
        return jnp.moveaxis(parts, 0, 1).reshape(batch, length, width)

    grad_key = totals[0].astype(jnp.bfloat16).reshape(batch, length, width)
    grad_value = totals[1].astype(jnp.bfloat16).reshape(batch, length, width)
    return (joined(pieces[0]), joined(pieces[1]), grad_key, grad_value)


def general_shards(queries, keys, values, out_weight, cotangent, block_mask):
    batch, tokens, width = queries.shape
    query_heads, key_heads, value_heads = (
        lax.all_to_all(queries, "seq", split_axis=2, concat_axis=1, tiled=True),
        lax.all_to_all(keys, "seq", split_axis=2, concat_axis=1, tiled=True),
        lax.all_to_all(values, "seq", split_axis=2, concat_axis=1, tiled=True),
    )
    weight_full = lax.all_gather(out_weight, "dp", axis=0, tiled=True)
    flat_cot = cotangent.reshape(batch * tokens, width)
    grad_attn = lax.dot_general(
        flat_cot, weight_full, (((1,), (1,)), ((), ())), preferred_element_type=jnp.float32
    )
    grad_attn = grad_attn.astype(jnp.bfloat16).reshape(batch, tokens, width)
    grad_heads = lax.all_to_all(grad_attn, "seq", split_axis=2, concat_axis=1, tiled=True)
    attended_heads, grad_q_heads, grad_k_heads, grad_v_heads = attend(
        query_heads, key_heads, value_heads, grad_heads, block_mask
    )
    attended, grad_queries, grad_keys, grad_values = (
        lax.all_to_all(attended_heads, "seq", split_axis=1, concat_axis=2, tiled=True),
        lax.all_to_all(grad_q_heads, "seq", split_axis=1, concat_axis=2, tiled=True),
        lax.all_to_all(grad_k_heads, "seq", split_axis=1, concat_axis=2, tiled=True),
        lax.all_to_all(grad_v_heads, "seq", split_axis=1, concat_axis=2, tiled=True),
    )
    flat_att = attended.reshape(batch * tokens, width)
    mixed = (
        jnp.dot(flat_att, weight_full, preferred_element_type=jnp.float32)
        .astype(jnp.bfloat16)
        .reshape(batch, tokens, width)
    )
    partial_grad = lax.psum_scatter(
        lax.dot_general(
            flat_att, flat_cot, (((0,), (0,)), ((), ())), preferred_element_type=jnp.float32
        ),
        "dp",
        scatter_dimension=0,
        tiled=True,
    )
    summed = lax.psum(partial_grad, "seq")
    grad_weight = summed / (batch * lax.axis_size("dp"))
    return (mixed, grad_queries, grad_keys, grad_values, grad_weight)


def fits_columns(mesh, queries, out_weight, block_mask):
    batch, length, width = queries
    return (
        mesh.shape["dp"] == 8
        and mesh.shape["seq"] == 4
        and batch == 8
        and length == 4 * DH
        and width == 16 * DH
        and out_weight == (width, width)
        and block_mask == (batch, 4, 4)
    )


def solution(mesh):
    placed = (
        P("dp", "seq", None),
        P("dp", "seq", None),
        P("dp", "seq", None),
        P("dp", None),
        P("dp", "seq", None),
        P("dp", None, None),
    )

    def program(queries, keys, values, out_weight, cotangent, block_mask):
        fits = fits_columns(mesh, queries.shape, out_weight.shape, block_mask.shape)
        return jax.shard_map(
            column_shards if fits else general_shards,
            mesh=mesh,
            in_specs=placed,
            out_specs=(
                P("dp", "seq", None),
                P("dp", "seq", None),
                P("dp", "seq", None),
                P("dp", "seq", None),
                P("dp", None),
            ),
            check_vma=False,
        )(queries, keys, values, out_weight, cotangent, block_mask)

    return program
```

```python
import math

import jax
import jax.numpy as jnp
from jax import lax
from jax.experimental import pallas as pl
from jax.experimental.pallas import tpu as pltpu
from jax.sharding import PartitionSpec as P

DH = 128
HALF = DH // 2
LOG2E = 1.4426950408889634
F32 = jnp.float32
BF16 = jnp.bfloat16
VMEM_BYTES = 20 * 1024 * 1024
HINT = 0


SMEM = pl.BlockSpec(memory_space=pltpu.SMEM)
VMEM = pl.BlockSpec(memory_space=pltpu.VMEM)
HBM = pl.BlockSpec(memory_space=pl.ANY)
FAR = pl.BlockSpec(memory_space=pltpu.HBM)


def call(kernel, name, operands, in_specs, out_shape, out_specs, scratch=(), hint=0, after=(), vmem=VMEM_BYTES):
    extra = len(after)

    def body(*refs):
        kernel(*refs[: len(operands)], *refs[len(operands) + extra :])

    return pl.pallas_call(
        body,
        in_specs=list(in_specs) + [HBM] * extra,
        out_specs=list(out_specs),
        out_shape=list(out_shape),
        scratch_shapes=list(scratch),
        compiler_params=pltpu.CompilerParams(vmem_limit_bytes=vmem),
        cost_estimate=pl.CostEstimate(flops=hint, bytes_accessed=1024, transcendentals=0),
        name=name,
    )(*operands, *after)


def run_copies(pairs, sems, first=0):
    copies = [pltpu.make_async_copy(s, d, sems.at[first + i]) for i, (s, d) in enumerate(pairs)]
    for copy in copies:
        copy.start()
    return copies


def head_columns(place, column, head):
    at = 4 * jnp.bitwise_xor(place[2], head) + column
    return pl.ds(pl.multiple_of(at * DH, DH), DH)


def block_rows(place, flip, tokens):
    return pl.ds(pl.multiple_of(jnp.bitwise_xor(place[0], flip) * tokens, tokens), tokens)


def split_kernel(place, query, key, value, out, held, sems):
    loads = run_copies([(source, held.at[index]) for index, source in enumerate((query, key, value))], sems)
    for index in range(3):
        loads[index].wait()
        for column in range(4):
            for h in range(4):
                out[column, index, :, h * DH : (h + 1) * DH] = held[index, :, head_columns(place, column, h)]


def split_heads(place, queries, keys, values, after=()):
    tokens, width = queries.shape
    out = jax.ShapeDtypeStruct((4, 3, tokens, width // 4), BF16)
    operands = (place, queries, keys, values)
    scratch = [pltpu.VMEM((3, tokens, width), BF16), pltpu.SemaphoreType.DMA((3,))]
    return call(split_kernel, "split_heads", operands, [SMEM] + [FAR] * 3, [out], [VMEM], scratch, after=after, vmem=3 * VMEM_BYTES)[0]


def chunk_kernel(place, own, got, chunk, part, sems):
    column, core = place[0], place[1]
    rows = pl.ds(pl.multiple_of((column % 2) * DH, DH), DH)
    owner = column // 2 == core
    pl.when(owner)(lambda: pltpu.make_async_copy(own.at[rows, :], chunk, sems.at[0]).start())
    pl.when(jnp.logical_not(owner))(lambda: pltpu.make_async_copy(got.at[rows, :], chunk, sems.at[0]).start())
    pltpu.make_async_copy(own.at[rows, :], chunk, sems.at[0]).wait()
    part[...] = chunk[pl.ds(pl.multiple_of(core * HALF, HALF), HALF), :]


def head_chunk(place, own, got, after=()):
    width = own.shape[1]
    out = [jax.ShapeDtypeStruct((rows, width), BF16) for rows in (DH, HALF)]
    scratch = [pltpu.SemaphoreType.DMA((1,))]
    return call(chunk_kernel, "head_chunk", (place, own, got), [SMEM, FAR, HBM], out, [VMEM] * 2, scratch, after=after)


def merge_kernel(place, blocks, *outs):
    for column in range(4):
        for index, target in enumerate(outs):
            for h in range(4):
                target[:, head_columns(place, column, h)] = blocks[column, index, :, h * DH : (h + 1) * DH]


def merge_heads(place, blocks, after=()):
    _, _, tokens, part = blocks.shape
    out = jax.ShapeDtypeStruct((tokens, 4 * part), BF16)
    return call(merge_kernel, "merge_heads", (place, blocks), [SMEM, VMEM], [out] * 3, [VMEM] * 3, after=after)


def dot(a, b, a_dim, b_dim):
    return lax.dot_general(a, b, (((a_dim,), (b_dim,)), ((), ())), preferred_element_type=F32)


def head_lanes(h):
    return pl.ds(h * DH, DH)


def load_heads(blocks, rows, sems):
    tokens = blocks.shape[2]
    return run_copies([(blocks.at[p], rows.at[:, pl.ds(p * tokens, tokens), :]) for p in range(4)], sems)


def load_pieces(pairs, sems, first, count):
    step = pairs[0][0].shape[1] // count
    copies = []
    for i in range(count):
        columns = pl.ds(i * step, step)
        copies.append(run_copies([(s.at[:, columns], d(columns)) for s, d in pairs], sems, first + i * len(pairs)))
    return copies


def cot_pairs(place, blocks, rows):
    tokens = blocks[0].shape[0]

    def target(flip, offset, count):
        start = pl.multiple_of(jnp.bitwise_xor(place[0], flip) * tokens + offset, HALF)
        return lambda columns: rows.at[pl.ds(start, count), columns]

    pairs = [(b, target(p, 0, tokens)) for p, b in enumerate(blocks[:3])]
    return pairs + [(b, target(3, i * (tokens // 2), tokens // 2)) for i, b in enumerate(blocks[3:])]


def slab_pairs(place, weights, slab):
    own, direct, crossed, half, other_half = weights
    core = place[1]

    def target(start, count):
        return lambda columns: slab.at[pl.ds(pl.multiple_of(start, HALF), count), columns]

    return [
        (own, target(0, DH)),
        (direct, target((1 + core) * DH, DH)),
        (crossed, target((2 - core) * DH, DH)),
        (half, target(3 * DH + core * HALF, HALF)),
        (other_half, target(3 * DH + (1 - core) * HALF, HALF)),
    ]


def wait_all(copies):
    for copy in copies:
        copy.wait()


def bias_rows(mask):
    rows = []
    for r in range(4):
        row = []
        for p in range(4):
            kept = mask[p * 4 + r] > 0
            row.append(jnp.full((1, DH), jnp.where(kept, 0.0, -1e30), F32))
        rows.append(jnp.concatenate(row, axis=1))
    return rows


def scores_kq(bias, query, key):
    raw = dot(key, query, 1, 1) * (LOG2E / math.sqrt(DH))
    return jnp.concatenate([raw[r * DH : (r + 1) * DH] + bias[r] for r in range(4)], axis=0)


def arrived_kernel(*refs):
    refs[-1][...] = jnp.zeros_like(refs[-1])


def arrived(arrays):
    out = jax.ShapeDtypeStruct((8, DH), F32)
    return call(arrived_kernel, "arrived", arrays, [HBM] * len(arrays), [out], [VMEM], hint=12_000_000_000)[0]


def forward_kernel(mask, blocks, attended, attended_t, log_total, qkv, sems):
    copies = load_heads(blocks, qkv, sems)
    bias = bias_rows(mask)
    wait_all(copies)
    for h in range(4):
        here = slice(h * DH, (h + 1) * DH)
        scores = scores_kq(bias, qkv[0, :, here], qkv[1, :, here])
        highest = jnp.max(scores, axis=0, keepdims=True)
        weights = jnp.exp2(scores - highest)
        total = jnp.sum(weights, axis=0, keepdims=True)
        rounded = (weights * (1.0 / total)).astype(BF16)
        out_t = dot(qkv[2, :, here], rounded, 0, 0).astype(BF16)
        attended_t[here, :] = out_t
        attended[:, here] = out_t.T
        log_total[h : h + 1, :] = highest + jnp.log2(total)


def forward(mask, blocks, after=()):
    _, _, tokens, part = blocks.shape
    length = 4 * tokens
    return call(
        forward_kernel,
        "forward",
        (mask, blocks),
        [SMEM, HBM],
        [
            jax.ShapeDtypeStruct((length, part), BF16),
            jax.ShapeDtypeStruct((part, length), BF16),
            jax.ShapeDtypeStruct((4, length), F32),
        ],
        [VMEM] * 3,
        [pltpu.VMEM((3, length, part), BF16), pltpu.SemaphoreType.DMA((4,))],
        after=after,
    )


def mixed_kernel(place, w0, w1, w2, w3, w4, attended, send_x, send_y, own, x_right, y_left, slab, total, sems):
    wait_all(load_pieces(slab_pairs(place, (w0, w1, w2, w3, w4), slab), sems, 0, 1)[0])
    tokens = attended.shape[0] // 4
    step = slab.shape[1] // 4
    for piece in range(4):
        columns = slice(piece * step, (piece + 1) * step)
        here = slice((piece % 2) * step, (piece % 2 + 1) * step)
        total[piece % 2] = dot(attended[...], slab[:, columns], 1, 0).astype(BF16)
        parts = [total.at[piece % 2][block_rows(place, flip, tokens), :] for flip in range(4)]
        own[:, columns] = parts[0]
        if piece < 2:
            send_x[0, :, here] = parts[1]
            send_x[1, :, here] = parts[3]
            y_left[:, here] = parts[2]
        else:
            send_y[0, :, here] = parts[2]
            send_y[1, :, here] = parts[3]
            x_right[:, here] = parts[1]


def mixed_parts(place, weights, attended, after=()):
    length, part = attended.shape
    width = weights[0].shape[1]
    tokens, half = length // 4, width // 2
    return call(
        mixed_kernel,
        "mixed_parts",
        (place, *weights, attended),
        [SMEM] + [HBM] * 5 + [VMEM],
        [
            jax.ShapeDtypeStruct((2, tokens, half), BF16),
            jax.ShapeDtypeStruct((2, tokens, half), BF16),
            jax.ShapeDtypeStruct((tokens, width), BF16),
            jax.ShapeDtypeStruct((tokens, half), BF16),
            jax.ShapeDtypeStruct((tokens, half), BF16),
        ],
        [VMEM] * 5,
        [
            pltpu.VMEM((part, width), BF16),
            pltpu.VMEM((2, length, width // 4), BF16),
            pltpu.SemaphoreType.DMA((5,)),
        ],
        after=after,
    )


def second_kernel(x_right, y_left, got_x, got_y, left, right):
    left[...] = (y_left[...].astype(F32) + got_x[1].astype(F32)).astype(BF16)
    right[...] = (x_right[...].astype(F32) + got_y[1].astype(F32)).astype(BF16)


def second_parts(x_right, y_left, got_x, got_y, after=()):
    out = jax.ShapeDtypeStruct(x_right.shape, BF16)
    operands = (x_right, y_left, got_x, got_y)
    return call(second_kernel, "second_parts", operands, [VMEM] * 4, [out] * 2, [VMEM] * 2, hint=HINT, after=after)


def weight_kernel(place, attended_t, c0, c1, c2, c3, c4, keep, send, cots, kept, sent, sems):
    loads = load_pieces(cot_pairs(place, (c0, c1, c2, c3, c4), cots), sems, 0, 1)[0]
    core = place[1]
    rows = []
    for half in (1 - core, core):
        for h in range(4):
            rows.append(attended_t[pl.ds(pl.multiple_of(h * DH + half * HALF, HALF), HALF), :])
    left = jnp.concatenate(rows, axis=0)
    step = cots.shape[1] // 4
    stores = []
    wait_all(loads)
    for piece in range(4):
        columns = slice(piece * step, (piece + 1) * step)
        total = dot(left, cots[:, columns], 1, 0).astype(BF16)
        for h in range(4):
            sent[h, :, columns] = total[h * HALF : (h + 1) * HALF]
            kept[h, :, columns] = total[(4 + h) * HALF : (5 + h) * HALF]
        window = pl.ds(piece * step, step)
        pairs = [(sent.at[:, :, window], send.at[:, :, window]), (kept.at[:, :, window], keep.at[:, :, window])]
        stores += run_copies(pairs, sems, 5 + 2 * piece)
    wait_all(stores)


def weight_parts(place, attended_t, cot_blocks, after=()):
    part, length = attended_t.shape
    width = cot_blocks[0].shape[1]
    out = jax.ShapeDtypeStruct((4, HALF, width), BF16)
    return call(
        weight_kernel,
        "weight_parts",
        (place, attended_t, *cot_blocks),
        [SMEM, VMEM] + [HBM] * 5,
        [out] * 2,
        [HBM] * 2,
        [
            pltpu.VMEM((length, width), BF16),
            pltpu.VMEM((4, HALF, width), BF16),
            pltpu.VMEM((4, HALF, width), BF16),
            pltpu.SemaphoreType.DMA((13,)),
        ],
        after=after,
    )


def add_kernel(keep, got, *outs):
    for h, out in enumerate(outs):
        out[...] = (keep[h].astype(F32) + got[h].astype(F32)).astype(BF16)


def add_cores(keep, got, after=()):
    out = jax.ShapeDtypeStruct(keep.shape[1:], BF16)
    return call(add_kernel, "add_cores", (keep, got), [VMEM] * 2, [out] * 4, [VMEM] * 4, after=after)


def sum_kernel(p0, p1, p2, p3, out):
    out[...] = (p0[...].astype(F32) + p1[...].astype(F32) + p2[...].astype(F32) + p3[...].astype(F32)).astype(BF16)


def sum_planes(*parts):
    out = jax.ShapeDtypeStruct(parts[0].shape, BF16)
    return call(sum_kernel, "sum_planes", parts, [VMEM] * 4, [out], [VMEM], hint=0)[0]


def weight_out_kernel(place, p0, p1, p2, p3, out):
    for k, piece in enumerate((p0, p1, p2, p3)):
        head = jnp.bitwise_xor(place[0] % 2, k % 2)
        half = jnp.bitwise_xor(jnp.bitwise_xor(place[1], place[0] // 2), k // 2)
        start = pl.multiple_of(head * DH + half * HALF, HALF)
        out[pl.ds(start, HALF), :] = piece[...].astype(F32) * 0.125


def weight_out(place, pieces, after=()):
    rows, width = pieces[0].shape
    out = jax.ShapeDtypeStruct((4 * rows, width), F32)
    return call(weight_out_kernel, "weight_out", (place, *pieces), [SMEM] + [VMEM] * 4, [out], [VMEM], after=after)[0]


def grads_kernel(place, w0, w1, w2, w3, w4, c0, c1, c2, c3, c4, grads, slab, cots, sems):
    loads = load_pieces(slab_pairs(place, (w0, w1, w2, w3, w4), slab), sems, 0, 1)
    loads += load_pieces(cot_pairs(place, (c0, c1, c2, c3, c4), cots), sems, 5, 1)
    wait_all(loads[0] + loads[1])
    for pair in range(2):
        rows = slice(pair * 2 * DH, (pair + 1) * 2 * DH)
        grads[:, rows] = dot(cots[...], slab[rows, :], 1, 1).astype(BF16)


def attended_grads(place, weights, cot_blocks, after=()):
    tokens, width = cot_blocks[0].shape
    part, length = 4 * DH, 4 * tokens
    return call(
        grads_kernel,
        "attended_grads",
        (place, *weights, *cot_blocks),
        [SMEM] + [HBM] * 10,
        [jax.ShapeDtypeStruct((length, part), BF16)],
        [VMEM],
        [
            pltpu.VMEM((part, width), BF16),
            pltpu.VMEM((length, width), BF16),
            pltpu.SemaphoreType.DMA((10,)),
        ],
        after=after,
    )[0]


def backward_kernel(mask, log_total, grads, blocks, out, qkv, made, sems):
    loads = load_heads(blocks, qkv, sems)
    tokens = out.shape[2]
    scale = 1.0 / math.sqrt(DH)
    bias = bias_rows(mask)
    stores = []
    wait_all(loads)
    for h in range(4):
        here = slice(h * DH, (h + 1) * DH)
        query, key, value, grad = qkv[0, :, here], qkv[1, :, here], qkv[2, :, here], grads[:, here]
        probs = jnp.exp2(scores_kq(bias, query, key) - log_total[h : h + 1, :])
        grad_value = dot(probs.astype(BF16), grad, 1, 0).astype(BF16)
        grad_probs = dot(value, grad, 1, 1)
        delta = jnp.sum(probs * grad_probs, axis=0, keepdims=True)
        grad_scores = (probs * (grad_probs - delta) * scale).astype(BF16)
        grad_key = dot(grad_scores, query, 1, 0).astype(BF16)
        grad_query = dot(key, grad_scores, 0, 0).astype(BF16).T
        for index, full in enumerate((grad_query, grad_key, grad_value)):
            for p in range(4):
                made[p, index, :, here] = full[p * tokens : (p + 1) * tokens]
        stores += run_copies([(made.at[:, :, :, head_lanes(h)], out.at[:, :, :, head_lanes(h)])], sems, 4 + h)
    wait_all(stores)


def backward(mask, log_total, grads, blocks, after=()):
    _, _, tokens, part = blocks.shape
    length = 4 * tokens
    return call(
        backward_kernel,
        "backward",
        (mask, log_total, grads, blocks),
        [SMEM] + [VMEM] * 2 + [HBM],
        [jax.ShapeDtypeStruct(blocks.shape, BF16)],
        [HBM],
        [pltpu.VMEM((3, length, part), BF16), pltpu.VMEM(blocks.shape, BF16), pltpu.SemaphoreType.DMA((8,))],
        after=after,
    )[0]


def column_shards(queries, keys, values, out_weight, cotangent, block_mask):
    tokens, width = queries.shape[1:]
    column = lax.axis_index("seq")
    rank = lax.axis_index("dp")
    core, z = rank % 2, rank // 2
    place = jnp.stack([column, core, z]).astype(jnp.int32)
    mask = block_mask.reshape(-1)
    cot = cotangent[0]

    def plane(array, flip):
        return lax.ppermute(array, "seq", [(i, i ^ flip) for i in range(4)])

    def swap(array):
        return lax.ppermute(array, "dp", [(i, i ^ 1) for i in range(8)])

    def along(array, flip):
        return lax.ppermute(array, "dp", [(i, i ^ (2 * flip)) for i in range(8)])

    def columns(array):
        return lax.all_to_all(array, "seq", 0, 0, tiled=True)

    heads = split_heads(place, queries[0], keys[0], values[0])
    blocks = columns(heads)

    cot_x, cot_y = plane(cot, 1), plane(cot, 2)

    def in_dp(array, target):
        return lax.ppermute(array, "dp", [(2 * a + c, target(a, c)) for a in range(4) for c in range(2)])

    chunk, part = head_chunk(place, out_weight, swap(out_weight), after=(heads,))
    direct = in_dp(chunk, lambda a, c: 2 * (a ^ (1 + c)) + c)
    part = in_dp(part, lambda a, c: 2 * (a ^ 3) + c)

    half = tokens // 2
    cot_blocks = (cot, cot_x, cot_y, plane(cot_y[:half], 1), plane(cot_x[half:], 2))
    attended, attended_t, log_total = forward(mask, blocks, after=(arrived((cot_x, cot_y)),))

    crossed, other, attended, far_y, far_x = lax.optimization_barrier((swap(direct), swap(part), attended, *cot_blocks[3:]))
    cot_blocks = (*cot_blocks[:3], far_y, far_x)
    weights = (chunk, direct, crossed, part, other)

    send_x, send_y, mixed_own, x_right, y_left = mixed_parts(place, weights, attended)
    got_x, got_y = plane(send_x, 1), plane(send_y, 2)

    keep, send = weight_parts(place, attended_t, cot_blocks, after=(send_x,))
    grads = attended_grads(place, weights, cot_blocks, after=(keep,))
    s0, s1, s2, s3 = add_cores(keep, swap(send), after=(grads,))
    got = [along(s, flip).astype(F32) for flip, s in ((1, s1), (2, s2), (3, s3))]
    summed = (s0.astype(F32) + got[0] + got[1] + got[2]).astype(BF16)
    made = backward(mask, log_total, grads, blocks, after=(s1,))
    outs = columns(made)
    left, right = second_parts(x_right, y_left, got_x, got_y, after=(made,))
    got_left, got_right = plane(left, 2), plane(right, 1)
    mixed = jnp.concatenate(
        [
            mixed_own[:, : width // 2].astype(F32) + got_x[0].astype(F32) + got_left.astype(F32),
            mixed_own[:, width // 2 :].astype(F32) + got_y[0].astype(F32) + got_right.astype(F32),
        ],
        axis=1,
    ).astype(BF16)

    pieces = []
    for k in range(4):
        pairs = []
        for plane_at in range(4):
            for c in range(2):
                for t in range(4):
                    to_core, to_column = t // 2, t ^ (2 * c) ^ k
                    pairs.append(((2 * plane_at + c) * 4 + t, (2 * plane_at + to_core) * 4 + to_column))
        pieces.append(lax.ppermute(summed, ("dp", "seq"), pairs))
    merged = merge_heads(place, outs, after=(summed, mixed))
    grad_weight = weight_out(place, pieces, after=(merged[0],))
    return (mixed[None],) + tuple(g[None] for g in merged) + (grad_weight,)


def attend(query_heads, key_heads, value_heads, grad_heads, block_mask):
    batch, length, width = query_heads.shape
    heads = width // DH
    shape_split = (batch, length, heads, DH)
    query_split = query_heads.reshape(shape_split)
    key_split = key_heads.reshape(shape_split)
    value_split = value_heads.reshape(shape_split)
    grad_split = grad_heads.reshape(shape_split)
    block = length // block_mask.shape[2]
    rows_step = min(512, length)
    scale = 1.0 / math.sqrt(DH)

    def step(carry, index):
        key_total, value_total = carry
        start = index * rows_step
        query_part = lax.dynamic_slice_in_dim(query_split, start, rows_step, 1)
        grad_part = lax.dynamic_slice_in_dim(grad_split, start, rows_step, 1)
        mask_part = lax.dynamic_slice_in_dim(block_mask, start // block, rows_step // block, 1)
        allowed = jnp.repeat(jnp.repeat(mask_part, block, axis=1), block, axis=2) > 0
        scores = (
            jnp.einsum("bqhd,bkhd->bhqk", query_part, key_split, preferred_element_type=jnp.float32)
            * scale
        )
        scores = jnp.where(allowed[:, None], scores, -1e30)
        highest = jnp.max(scores, axis=3, keepdims=True)
        log_total = highest + jnp.log(jnp.sum(jnp.exp(scores - highest), axis=3, keepdims=True))
        probs = jnp.exp(scores - log_total)
        rounded = probs.astype(jnp.bfloat16)
        attended = jnp.einsum(
            "bhqk,bkhd->bqhd", rounded, value_split, preferred_element_type=jnp.float32
        ).astype(jnp.bfloat16)
        value_total = value_total + jnp.einsum(
            "bhqk,bqhd->bkhd", rounded, grad_part, preferred_element_type=jnp.float32
        )
        grad_probs = jnp.einsum(
            "bqhd,bkhd->bhqk", grad_part, value_split, preferred_element_type=jnp.float32
        )
        delta = jnp.sum(probs * grad_probs, axis=3, keepdims=True)
        grad_scores = (probs * (grad_probs - delta) * scale).astype(jnp.bfloat16)
        grad_query = jnp.einsum(
            "bhqk,bkhd->bqhd", grad_scores, key_split, preferred_element_type=jnp.float32
        ).astype(jnp.bfloat16)
        key_total = key_total + jnp.einsum(
            "bhqk,bqhd->bkhd", grad_scores, query_part, preferred_element_type=jnp.float32
        )
        return ((key_total, value_total), (attended, grad_query))

    zeros = jnp.zeros(shape_split, jnp.float32)
    totals, pieces = lax.scan(
        step, (zeros, zeros), jnp.arange(length // rows_step, dtype=jnp.int32)
    )

    def joined(parts):
        return jnp.moveaxis(parts, 0, 1).reshape(batch, length, width)

    grad_key = totals[0].astype(jnp.bfloat16).reshape(batch, length, width)
    grad_value = totals[1].astype(jnp.bfloat16).reshape(batch, length, width)
    return (joined(pieces[0]), joined(pieces[1]), grad_key, grad_value)


def general_shards(queries, keys, values, out_weight, cotangent, block_mask):
    batch, tokens, width = queries.shape
    query_heads, key_heads, value_heads = (
        lax.all_to_all(queries, "seq", split_axis=2, concat_axis=1, tiled=True),
        lax.all_to_all(keys, "seq", split_axis=2, concat_axis=1, tiled=True),
        lax.all_to_all(values, "seq", split_axis=2, concat_axis=1, tiled=True),
    )
    weight_full = lax.all_gather(out_weight, "dp", axis=0, tiled=True)
    flat_cot = cotangent.reshape(batch * tokens, width)
    grad_attn = lax.dot_general(
        flat_cot, weight_full, (((1,), (1,)), ((), ())), preferred_element_type=jnp.float32
    )
    grad_attn = grad_attn.astype(jnp.bfloat16).reshape(batch, tokens, width)
    grad_heads = lax.all_to_all(grad_attn, "seq", split_axis=2, concat_axis=1, tiled=True)
    attended_heads, grad_q_heads, grad_k_heads, grad_v_heads = attend(
        query_heads, key_heads, value_heads, grad_heads, block_mask
    )
    attended, grad_queries, grad_keys, grad_values = (
        lax.all_to_all(attended_heads, "seq", split_axis=1, concat_axis=2, tiled=True),
        lax.all_to_all(grad_q_heads, "seq", split_axis=1, concat_axis=2, tiled=True),
        lax.all_to_all(grad_k_heads, "seq", split_axis=1, concat_axis=2, tiled=True),
        lax.all_to_all(grad_v_heads, "seq", split_axis=1, concat_axis=2, tiled=True),
    )
    flat_att = attended.reshape(batch * tokens, width)
    mixed = (
        jnp.dot(flat_att, weight_full, preferred_element_type=jnp.float32)
        .astype(jnp.bfloat16)
        .reshape(batch, tokens, width)
    )
    partial_grad = lax.psum_scatter(
        lax.dot_general(
            flat_att, flat_cot, (((0,), (0,)), ((), ())), preferred_element_type=jnp.float32
        ),
        "dp",
        scatter_dimension=0,
        tiled=True,
    )
    summed = lax.psum(partial_grad, "seq")
    grad_weight = summed / (batch * lax.axis_size("dp"))
    return (mixed, grad_queries, grad_keys, grad_values, grad_weight)


def fits_columns(mesh, queries, out_weight, block_mask):
    batch, length, width = queries
    return (
        mesh.shape["dp"] == 8
        and mesh.shape["seq"] == 4
        and batch == 8
        and length == 4 * DH
        and width == 16 * DH
        and out_weight == (width, width)
        and block_mask == (batch, 4, 4)
    )


def solution(mesh):
    placed = (
        P("dp", "seq", None),
        P("dp", "seq", None),
        P("dp", "seq", None),
        P("dp", None),
        P("dp", "seq", None),
        P("dp", None, None),
    )

    def program(queries, keys, values, out_weight, cotangent, block_mask):
        fits = fits_columns(mesh, queries.shape, out_weight.shape, block_mask.shape)
        return jax.shard_map(
            column_shards if fits else general_shards,
            mesh=mesh,
            in_specs=placed,
            out_specs=(
                P("dp", "seq", None),
                P("dp", "seq", None),
                P("dp", "seq", None),
                P("dp", "seq", None),
                P("dp", None),
            ),
            check_vma=False,
        )(queries, keys, values, out_weight, cotangent, block_mask)

    return program
```

```python
import math

import jax
import jax.numpy as jnp
from jax import lax
from jax.experimental import pallas as pl
from jax.experimental.pallas import tpu as pltpu
from jax.sharding import PartitionSpec as P

DH = 128
HALF = DH // 2
LOG2E = 1.4426950408889634
F32 = jnp.float32
BF16 = jnp.bfloat16
VMEM_BYTES = 20 * 1024 * 1024
HINT = 2_000_000_000


SMEM = pl.BlockSpec(memory_space=pltpu.SMEM)
VMEM = pl.BlockSpec(memory_space=pltpu.VMEM)
HBM = pl.BlockSpec(memory_space=pl.ANY)
FAR = pl.BlockSpec(memory_space=pltpu.HBM)


def call(kernel, name, operands, in_specs, out_shape, out_specs, scratch=(), hint=0, after=(), vmem=VMEM_BYTES):
    extra = len(after)

    def body(*refs):
        kernel(*refs[: len(operands)], *refs[len(operands) + extra :])

    return pl.pallas_call(
        body,
        in_specs=list(in_specs) + [HBM] * extra,
        out_specs=list(out_specs),
        out_shape=list(out_shape),
        scratch_shapes=list(scratch),
        compiler_params=pltpu.CompilerParams(vmem_limit_bytes=vmem),
        cost_estimate=pl.CostEstimate(flops=hint, bytes_accessed=1024, transcendentals=0),
        name=name,
    )(*operands, *after)


def run_copies(pairs, sems, first=0):
    copies = [pltpu.make_async_copy(s, d, sems.at[first + i]) for i, (s, d) in enumerate(pairs)]
    for copy in copies:
        copy.start()
    return copies


def head_columns(place, column, head):
    at = 4 * jnp.bitwise_xor(place[2], head) + column
    return pl.ds(pl.multiple_of(at * DH, DH), DH)


def block_rows(place, flip, tokens):
    return pl.ds(pl.multiple_of(jnp.bitwise_xor(place[0], flip) * tokens, tokens), tokens)


def split_kernel(place, query, key, value, out, held, sems):
    loads = run_copies([(source, held.at[index]) for index, source in enumerate((query, key, value))], sems)
    for index in range(3):
        loads[index].wait()
        for column in range(4):
            for h in range(4):
                out[column, index, :, h * DH : (h + 1) * DH] = held[index, :, head_columns(place, column, h)]


def split_heads(place, queries, keys, values, after=()):
    tokens, width = queries.shape
    out = jax.ShapeDtypeStruct((4, 3, tokens, width // 4), BF16)
    operands = (place, queries, keys, values)
    scratch = [pltpu.VMEM((3, tokens, width), BF16), pltpu.SemaphoreType.DMA((3,))]
    return call(split_kernel, "split_heads", operands, [SMEM] + [FAR] * 3, [out], [VMEM], scratch, after=after, vmem=3 * VMEM_BYTES)[0]


def chunk_kernel(place, own, got, chunk, part, sems):
    column, core = place[0], place[1]
    rows = pl.ds(pl.multiple_of((column % 2) * DH, DH), DH)
    owner = column // 2 == core
    pl.when(owner)(lambda: pltpu.make_async_copy(own.at[rows, :], chunk, sems.at[0]).start())
    pl.when(jnp.logical_not(owner))(lambda: pltpu.make_async_copy(got.at[rows, :], chunk, sems.at[0]).start())
    pltpu.make_async_copy(own.at[rows, :], chunk, sems.at[0]).wait()
    part[...] = chunk[pl.ds(pl.multiple_of(core * HALF, HALF), HALF), :]


def head_chunk(place, own, got, after=()):
    width = own.shape[1]
    out = [jax.ShapeDtypeStruct((rows, width), BF16) for rows in (DH, HALF)]
    scratch = [pltpu.SemaphoreType.DMA((1,))]
    return call(chunk_kernel, "head_chunk", (place, own, got), [SMEM, FAR, HBM], out, [VMEM] * 2, scratch, after=after)


def merge_kernel(place, blocks, *outs):
    *outs, token = outs
    token[...] = jnp.zeros_like(token)
    for column in range(4):
        for index, target in enumerate(outs):
            for h in range(4):
                target[:, head_columns(place, column, h)] = blocks[column, index, :, h * DH : (h + 1) * DH]


def merge_heads(place, blocks, after=()):
    _, _, tokens, part = blocks.shape
    out = jax.ShapeDtypeStruct((tokens, 4 * part), BF16)
    token = jax.ShapeDtypeStruct((8, DH), F32)
    return call(merge_kernel, "merge_heads", (place, blocks), [SMEM, VMEM], [out] * 3 + [token], [VMEM] * 4, after=after)


def dot(a, b, a_dim, b_dim):
    return lax.dot_general(a, b, (((a_dim,), (b_dim,)), ((), ())), preferred_element_type=F32)


def head_lanes(h):
    return pl.ds(h * DH, DH)


def load_heads(blocks, rows, sems):
    tokens = blocks.shape[2]
    return run_copies([(blocks.at[p], rows.at[:, pl.ds(p * tokens, tokens), :]) for p in range(4)], sems)


def load_pieces(pairs, sems, first, count):
    step = pairs[0][0].shape[1] // count
    copies = []
    for i in range(count):
        columns = pl.ds(i * step, step)
        copies.append(run_copies([(s.at[:, columns], d(columns)) for s, d in pairs], sems, first + i * len(pairs)))
    return copies


def cot_pairs(place, blocks, rows):
    tokens = blocks[0].shape[0]

    def target(flip, offset, count):
        start = pl.multiple_of(jnp.bitwise_xor(place[0], flip) * tokens + offset, HALF)
        return lambda columns: rows.at[pl.ds(start, count), columns]

    pairs = [(b, target(p, 0, tokens)) for p, b in enumerate(blocks[:3])]
    return pairs + [(b, target(3, i * (tokens // 2), tokens // 2)) for i, b in enumerate(blocks[3:])]


def slab_pairs(place, weights, slab):
    own, direct, crossed, half, other_half = weights
    core = place[1]

    def target(start, count):
        return lambda columns: slab.at[pl.ds(pl.multiple_of(start, HALF), count), columns]

    return [
        (own, target(0, DH)),
        (direct, target((1 + core) * DH, DH)),
        (crossed, target((2 - core) * DH, DH)),
        (half, target(3 * DH + core * HALF, HALF)),
        (other_half, target(3 * DH + (1 - core) * HALF, HALF)),
    ]


def wait_all(copies):
    for copy in copies:
        copy.wait()


def bias_rows(mask):
    rows = []
    for r in range(4):
        row = []
        for p in range(4):
            kept = mask[p * 4 + r] > 0
            row.append(jnp.full((1, DH), jnp.where(kept, 0.0, -1e30), F32))
        rows.append(jnp.concatenate(row, axis=1))
    return rows


def scores_kq(bias, query, key):
    raw = dot(key, query, 1, 1) * (LOG2E / math.sqrt(DH))
    return jnp.concatenate([raw[r * DH : (r + 1) * DH] + bias[r] for r in range(4)], axis=0)


def arrived_kernel(*refs):
    refs[-1][...] = jnp.zeros_like(refs[-1])


def arrived(arrays):
    out = jax.ShapeDtypeStruct((8, DH), F32)
    return call(arrived_kernel, "arrived", arrays, [HBM] * len(arrays), [out], [VMEM], hint=12_000_000_000)[0]


def forward_kernel(mask, blocks, attended, attended_t, log_total, qkv, sems):
    copies = load_heads(blocks, qkv, sems)
    bias = bias_rows(mask)
    wait_all(copies)
    for h in range(4):
        here = slice(h * DH, (h + 1) * DH)
        scores = scores_kq(bias, qkv[0, :, here], qkv[1, :, here])
        highest = jnp.max(scores, axis=0, keepdims=True)
        weights = jnp.exp2(scores - highest)
        total = jnp.sum(weights, axis=0, keepdims=True)
        rounded = (weights * (1.0 / total)).astype(BF16)
        out_t = dot(qkv[2, :, here], rounded, 0, 0).astype(BF16)
        attended_t[here, :] = out_t
        attended[:, here] = out_t.T
        log_total[h : h + 1, :] = highest + jnp.log2(total)


def forward(mask, blocks, after=()):
    _, _, tokens, part = blocks.shape
    length = 4 * tokens
    return call(
        forward_kernel,
        "forward",
        (mask, blocks),
        [SMEM, HBM],
        [
            jax.ShapeDtypeStruct((length, part), BF16),
            jax.ShapeDtypeStruct((part, length), BF16),
            jax.ShapeDtypeStruct((4, length), F32),
        ],
        [VMEM] * 3,
        [pltpu.VMEM((3, length, part), BF16), pltpu.SemaphoreType.DMA((4,))],
        after=after,
    )


def mixed_kernel(place, w0, w1, w2, w3, w4, attended, send_x, send_y, own, x_right, y_left, slab, total, sems):
    wait_all(load_pieces(slab_pairs(place, (w0, w1, w2, w3, w4), slab), sems, 0, 1)[0])
    tokens = attended.shape[0] // 4
    step = slab.shape[1] // 4
    for piece in range(4):
        columns = slice(piece * step, (piece + 1) * step)
        here = slice((piece % 2) * step, (piece % 2 + 1) * step)
        total[piece % 2] = dot(attended[...], slab[:, columns], 1, 0).astype(BF16)
        parts = [total.at[piece % 2][block_rows(place, flip, tokens), :] for flip in range(4)]
        own[:, columns] = parts[0]
        if piece < 2:
            send_x[0, :, here] = parts[1]
            send_x[1, :, here] = parts[3]
            y_left[:, here] = parts[2]
        else:
            send_y[0, :, here] = parts[2]
            send_y[1, :, here] = parts[3]
            x_right[:, here] = parts[1]


def mixed_parts(place, weights, attended, after=()):
    length, part = attended.shape
    width = weights[0].shape[1]
    tokens, half = length // 4, width // 2
    return call(
        mixed_kernel,
        "mixed_parts",
        (place, *weights, attended),
        [SMEM] + [HBM] * 5 + [VMEM],
        [
            jax.ShapeDtypeStruct((2, tokens, half), BF16),
            jax.ShapeDtypeStruct((2, tokens, half), BF16),
            jax.ShapeDtypeStruct((tokens, width), BF16),
            jax.ShapeDtypeStruct((tokens, half), BF16),
            jax.ShapeDtypeStruct((tokens, half), BF16),
        ],
        [VMEM] * 5,
        [
            pltpu.VMEM((part, width), BF16),
            pltpu.VMEM((2, length, width // 4), BF16),
            pltpu.SemaphoreType.DMA((5,)),
        ],
        after=after,
    )


def second_kernel(x_right, y_left, got_x, got_y, left, right):
    left[...] = (y_left[...].astype(F32) + got_x[1].astype(F32)).astype(BF16)
    right[...] = (x_right[...].astype(F32) + got_y[1].astype(F32)).astype(BF16)


def second_parts(x_right, y_left, got_x, got_y, after=()):
    out = jax.ShapeDtypeStruct(x_right.shape, BF16)
    operands = (x_right, y_left, got_x, got_y)
    return call(second_kernel, "second_parts", operands, [VMEM] * 4, [out] * 2, [VMEM] * 2, hint=HINT, after=after)


def weight_kernel(place, attended_t, c0, c1, c2, c3, c4, keep, send, cots, kept, sent, sems):
    loads = load_pieces(cot_pairs(place, (c0, c1, c2, c3, c4), cots), sems, 0, 1)[0]
    core = place[1]
    rows = []
    for half in (1 - core, core):
        for h in range(4):
            rows.append(attended_t[pl.ds(pl.multiple_of(h * DH + half * HALF, HALF), HALF), :])
    left = jnp.concatenate(rows, axis=0)
    step = cots.shape[1] // 4
    stores = []
    wait_all(loads)
    for piece in range(4):
        columns = slice(piece * step, (piece + 1) * step)
        total = dot(left, cots[:, columns], 1, 0).astype(BF16)
        for h in range(4):
            sent[h, :, columns] = total[h * HALF : (h + 1) * HALF]
            kept[h, :, columns] = total[(4 + h) * HALF : (5 + h) * HALF]
        window = pl.ds(piece * step, step)
        pairs = [(sent.at[:, :, window], send.at[:, :, window]), (kept.at[:, :, window], keep.at[:, :, window])]
        stores += run_copies(pairs, sems, 5 + 2 * piece)
    wait_all(stores)


def weight_parts(place, attended_t, cot_blocks, after=()):
    part, length = attended_t.shape
    width = cot_blocks[0].shape[1]
    out = jax.ShapeDtypeStruct((4, HALF, width), BF16)
    return call(
        weight_kernel,
        "weight_parts",
        (place, attended_t, *cot_blocks),
        [SMEM, VMEM] + [HBM] * 5,
        [out] * 2,
        [HBM] * 2,
        [
            pltpu.VMEM((length, width), BF16),
            pltpu.VMEM((4, HALF, width), BF16),
            pltpu.VMEM((4, HALF, width), BF16),
            pltpu.SemaphoreType.DMA((13,)),
        ],
        after=after,
    )


def add_kernel(keep, got, *outs):
    for h, out in enumerate(outs):
        out[...] = (keep[h].astype(F32) + got[h].astype(F32)).astype(BF16)


def add_cores(keep, got, after=()):
    out = jax.ShapeDtypeStruct(keep.shape[1:], BF16)
    return call(add_kernel, "add_cores", (keep, got), [VMEM] * 2, [out] * 4, [VMEM] * 4, after=after)


def sum_kernel(p0, p1, p2, p3, out):
    out[...] = (p0[...].astype(F32) + p1[...].astype(F32) + p2[...].astype(F32) + p3[...].astype(F32)).astype(BF16)


def sum_planes(*parts):
    out = jax.ShapeDtypeStruct(parts[0].shape, BF16)
    return call(sum_kernel, "sum_planes", parts, [VMEM] * 4, [out], [VMEM], hint=0)[0]


def weight_out_kernel(place, p0, p1, p2, p3, out):
    for k, piece in enumerate((p0, p1, p2, p3)):
        head = jnp.bitwise_xor(place[0] % 2, k % 2)
        half = jnp.bitwise_xor(jnp.bitwise_xor(place[1], place[0] // 2), k // 2)
        start = pl.multiple_of(head * DH + half * HALF, HALF)
        out[pl.ds(start, HALF), :] = piece[...].astype(F32) * 0.125


def weight_out(place, pieces, after=()):
    rows, width = pieces[0].shape
    out = jax.ShapeDtypeStruct((4 * rows, width), F32)
    return call(weight_out_kernel, "weight_out", (place, *pieces), [SMEM] + [VMEM] * 4, [out], [VMEM], after=after)[0]


def grads_kernel(place, w0, w1, w2, w3, w4, c0, c1, c2, c3, c4, grads, slab, cots, sems):
    loads = load_pieces(slab_pairs(place, (w0, w1, w2, w3, w4), slab), sems, 0, 1)
    loads += load_pieces(cot_pairs(place, (c0, c1, c2, c3, c4), cots), sems, 5, 1)
    wait_all(loads[0] + loads[1])
    for pair in range(2):
        rows = slice(pair * 2 * DH, (pair + 1) * 2 * DH)
        grads[:, rows] = dot(cots[...], slab[rows, :], 1, 1).astype(BF16)


def attended_grads(place, weights, cot_blocks, after=()):
    tokens, width = cot_blocks[0].shape
    part, length = 4 * DH, 4 * tokens
    return call(
        grads_kernel,
        "attended_grads",
        (place, *weights, *cot_blocks),
        [SMEM] + [HBM] * 10,
        [jax.ShapeDtypeStruct((length, part), BF16)],
        [VMEM],
        [
            pltpu.VMEM((part, width), BF16),
            pltpu.VMEM((length, width), BF16),
            pltpu.SemaphoreType.DMA((10,)),
        ],
        after=after,
    )[0]


def backward_kernel(mask, log_total, grads, blocks, out, qkv, made, sems):
    loads = load_heads(blocks, qkv, sems)
    tokens = out.shape[2]
    scale = 1.0 / math.sqrt(DH)
    bias = bias_rows(mask)
    stores = []
    wait_all(loads)
    for h in range(4):
        here = slice(h * DH, (h + 1) * DH)
        query, key, value, grad = qkv[0, :, here], qkv[1, :, here], qkv[2, :, here], grads[:, here]
        probs = jnp.exp2(scores_kq(bias, query, key) - log_total[h : h + 1, :])
        grad_value = dot(probs.astype(BF16), grad, 1, 0).astype(BF16)
        grad_probs = dot(value, grad, 1, 1)
        delta = jnp.sum(probs * grad_probs, axis=0, keepdims=True)
        grad_scores = (probs * (grad_probs - delta) * scale).astype(BF16)
        grad_key = dot(grad_scores, query, 1, 0).astype(BF16)
        grad_query = dot(key, grad_scores, 0, 0).astype(BF16).T
        for index, full in enumerate((grad_query, grad_key, grad_value)):
            for p in range(4):
                made[p, index, :, here] = full[p * tokens : (p + 1) * tokens]
        stores += run_copies([(made.at[:, :, :, head_lanes(h)], out.at[:, :, :, head_lanes(h)])], sems, 4 + h)
    wait_all(stores)


def backward(mask, log_total, grads, blocks, after=()):
    _, _, tokens, part = blocks.shape
    length = 4 * tokens
    return call(
        backward_kernel,
        "backward",
        (mask, log_total, grads, blocks),
        [SMEM] + [VMEM] * 2 + [HBM],
        [jax.ShapeDtypeStruct(blocks.shape, BF16)],
        [HBM],
        [pltpu.VMEM((3, length, part), BF16), pltpu.VMEM(blocks.shape, BF16), pltpu.SemaphoreType.DMA((8,))],
        after=after,
    )[0]


def column_shards(queries, keys, values, out_weight, cotangent, block_mask):
    tokens, width = queries.shape[1:]
    column = lax.axis_index("seq")
    rank = lax.axis_index("dp")
    core, z = rank % 2, rank // 2
    place = jnp.stack([column, core, z]).astype(jnp.int32)
    mask = block_mask.reshape(-1)
    cot = cotangent[0]

    def plane(array, flip):
        return lax.ppermute(array, "seq", [(i, i ^ flip) for i in range(4)])

    def swap(array):
        return lax.ppermute(array, "dp", [(i, i ^ 1) for i in range(8)])

    def along(array, flip):
        return lax.ppermute(array, "dp", [(i, i ^ (2 * flip)) for i in range(8)])

    def columns(array):
        return lax.all_to_all(array, "seq", 0, 0, tiled=True)

    heads = split_heads(place, queries[0], keys[0], values[0])
    blocks = columns(heads)

    cot_x, cot_y = plane(cot, 1), plane(cot, 2)

    def in_dp(array, target):
        return lax.ppermute(array, "dp", [(2 * a + c, target(a, c)) for a in range(4) for c in range(2)])

    chunk, part = head_chunk(place, out_weight, swap(out_weight), after=(heads,))
    direct = in_dp(chunk, lambda a, c: 2 * (a ^ (1 + c)) + c)
    part = in_dp(part, lambda a, c: 2 * (a ^ 3) + c)

    half = tokens // 2
    cot_blocks = (cot, cot_x, cot_y, plane(cot_y[:half], 1), plane(cot_x[half:], 2))
    attended, attended_t, log_total = forward(mask, blocks, after=(arrived((cot_x, cot_y)),))

    crossed, other, attended, far_y, far_x = lax.optimization_barrier((swap(direct), swap(part), attended, *cot_blocks[3:]))
    cot_blocks = (*cot_blocks[:3], far_y, far_x)
    weights = (chunk, direct, crossed, part, other)

    send_x, send_y, mixed_own, x_right, y_left = mixed_parts(place, weights, attended)
    got_x, got_y = plane(send_x, 1), plane(send_y, 2)

    keep, send = weight_parts(place, attended_t, cot_blocks, after=(send_x,))
    grads = attended_grads(place, weights, cot_blocks, after=(keep,))
    s0, s1, s2, s3 = add_cores(keep, swap(send), after=(grads,))
    got = [along(s, flip).astype(F32) for flip, s in ((1, s1), (2, s2), (3, s3))]
    summed = (s0.astype(F32) + got[0] + got[1] + got[2]).astype(BF16)
    made = backward(mask, log_total, grads, blocks, after=(s1,))
    outs = columns(made)
    left, right = second_parts(x_right, y_left, got_x, got_y, after=(made,))
    got_left, got_right = plane(left, 2), plane(right, 1)
    mixed = jnp.concatenate(
        [
            mixed_own[:, : width // 2].astype(F32) + got_x[0].astype(F32) + got_left.astype(F32),
            mixed_own[:, width // 2 :].astype(F32) + got_y[0].astype(F32) + got_right.astype(F32),
        ],
        axis=1,
    ).astype(BF16)

    pieces = []
    for k in range(4):
        pairs = []
        for plane_at in range(4):
            for c in range(2):
                for t in range(4):
                    to_core, to_column = t // 2, t ^ (2 * c) ^ k
                    pairs.append(((2 * plane_at + c) * 4 + t, (2 * plane_at + to_core) * 4 + to_column))
        pieces.append(lax.ppermute(summed, ("dp", "seq"), pairs))
    *merged, token = merge_heads(place, outs, after=(summed, mixed))
    grad_weight = weight_out(place, pieces, after=(token,))
    return (mixed[None],) + tuple(g[None] for g in merged) + (grad_weight,)


def attend(query_heads, key_heads, value_heads, grad_heads, block_mask):
    batch, length, width = query_heads.shape
    heads = width // DH
    shape_split = (batch, length, heads, DH)
    query_split = query_heads.reshape(shape_split)
    key_split = key_heads.reshape(shape_split)
    value_split = value_heads.reshape(shape_split)
    grad_split = grad_heads.reshape(shape_split)
    block = length // block_mask.shape[2]
    rows_step = min(512, length)
    scale = 1.0 / math.sqrt(DH)

    def step(carry, index):
        key_total, value_total = carry
        start = index * rows_step
        query_part = lax.dynamic_slice_in_dim(query_split, start, rows_step, 1)
        grad_part = lax.dynamic_slice_in_dim(grad_split, start, rows_step, 1)
        mask_part = lax.dynamic_slice_in_dim(block_mask, start // block, rows_step // block, 1)
        allowed = jnp.repeat(jnp.repeat(mask_part, block, axis=1), block, axis=2) > 0
        scores = (
            jnp.einsum("bqhd,bkhd->bhqk", query_part, key_split, preferred_element_type=jnp.float32)
            * scale
        )
        scores = jnp.where(allowed[:, None], scores, -1e30)
        highest = jnp.max(scores, axis=3, keepdims=True)
        log_total = highest + jnp.log(jnp.sum(jnp.exp(scores - highest), axis=3, keepdims=True))
        probs = jnp.exp(scores - log_total)
        rounded = probs.astype(jnp.bfloat16)
        attended = jnp.einsum(
            "bhqk,bkhd->bqhd", rounded, value_split, preferred_element_type=jnp.float32
        ).astype(jnp.bfloat16)
        value_total = value_total + jnp.einsum(
            "bhqk,bqhd->bkhd", rounded, grad_part, preferred_element_type=jnp.float32
        )
        grad_probs = jnp.einsum(
            "bqhd,bkhd->bhqk", grad_part, value_split, preferred_element_type=jnp.float32
        )
        delta = jnp.sum(probs * grad_probs, axis=3, keepdims=True)
        grad_scores = (probs * (grad_probs - delta) * scale).astype(jnp.bfloat16)
        grad_query = jnp.einsum(
            "bhqk,bkhd->bqhd", grad_scores, key_split, preferred_element_type=jnp.float32
        ).astype(jnp.bfloat16)
        key_total = key_total + jnp.einsum(
            "bhqk,bqhd->bkhd", grad_scores, query_part, preferred_element_type=jnp.float32
        )
        return ((key_total, value_total), (attended, grad_query))

    zeros = jnp.zeros(shape_split, jnp.float32)
    totals, pieces = lax.scan(
        step, (zeros, zeros), jnp.arange(length // rows_step, dtype=jnp.int32)
    )

    def joined(parts):
        return jnp.moveaxis(parts, 0, 1).reshape(batch, length, width)

    grad_key = totals[0].astype(jnp.bfloat16).reshape(batch, length, width)
    grad_value = totals[1].astype(jnp.bfloat16).reshape(batch, length, width)
    return (joined(pieces[0]), joined(pieces[1]), grad_key, grad_value)


def general_shards(queries, keys, values, out_weight, cotangent, block_mask):
    batch, tokens, width = queries.shape
    query_heads, key_heads, value_heads = (
        lax.all_to_all(queries, "seq", split_axis=2, concat_axis=1, tiled=True),
        lax.all_to_all(keys, "seq", split_axis=2, concat_axis=1, tiled=True),
        lax.all_to_all(values, "seq", split_axis=2, concat_axis=1, tiled=True),
    )
    weight_full = lax.all_gather(out_weight, "dp", axis=0, tiled=True)
    flat_cot = cotangent.reshape(batch * tokens, width)
    grad_attn = lax.dot_general(
        flat_cot, weight_full, (((1,), (1,)), ((), ())), preferred_element_type=jnp.float32
    )
    grad_attn = grad_attn.astype(jnp.bfloat16).reshape(batch, tokens, width)
    grad_heads = lax.all_to_all(grad_attn, "seq", split_axis=2, concat_axis=1, tiled=True)
    attended_heads, grad_q_heads, grad_k_heads, grad_v_heads = attend(
        query_heads, key_heads, value_heads, grad_heads, block_mask
    )
    attended, grad_queries, grad_keys, grad_values = (
        lax.all_to_all(attended_heads, "seq", split_axis=1, concat_axis=2, tiled=True),
        lax.all_to_all(grad_q_heads, "seq", split_axis=1, concat_axis=2, tiled=True),
        lax.all_to_all(grad_k_heads, "seq", split_axis=1, concat_axis=2, tiled=True),
        lax.all_to_all(grad_v_heads, "seq", split_axis=1, concat_axis=2, tiled=True),
    )
    flat_att = attended.reshape(batch * tokens, width)
    mixed = (
        jnp.dot(flat_att, weight_full, preferred_element_type=jnp.float32)
        .astype(jnp.bfloat16)
        .reshape(batch, tokens, width)
    )
    partial_grad = lax.psum_scatter(
        lax.dot_general(
            flat_att, flat_cot, (((0,), (0,)), ((), ())), preferred_element_type=jnp.float32
        ),
        "dp",
        scatter_dimension=0,
        tiled=True,
    )
    summed = lax.psum(partial_grad, "seq")
    grad_weight = summed / (batch * lax.axis_size("dp"))
    return (mixed, grad_queries, grad_keys, grad_values, grad_weight)


def fits_columns(mesh, queries, out_weight, block_mask):
    batch, length, width = queries
    return (
        mesh.shape["dp"] == 8
        and mesh.shape["seq"] == 4
        and batch == 8
        and length == 4 * DH
        and width == 16 * DH
        and out_weight == (width, width)
        and block_mask == (batch, 4, 4)
    )


def solution(mesh):
    placed = (
        P("dp", "seq", None),
        P("dp", "seq", None),
        P("dp", "seq", None),
        P("dp", None),
        P("dp", "seq", None),
        P("dp", None, None),
    )

    def program(queries, keys, values, out_weight, cotangent, block_mask):
        fits = fits_columns(mesh, queries.shape, out_weight.shape, block_mask.shape)
        return jax.shard_map(
            column_shards if fits else general_shards,
            mesh=mesh,
            in_specs=placed,
            out_specs=(
                P("dp", "seq", None),
                P("dp", "seq", None),
                P("dp", "seq", None),
                P("dp", "seq", None),
                P("dp", None),
            ),
            check_vma=False,
        )(queries, keys, values, out_weight, cotangent, block_mask)

    return program
```

```python
import math

import jax
import jax.numpy as jnp
from jax import lax
from jax.experimental import pallas as pl
from jax.experimental.pallas import tpu as pltpu
from jax.sharding import PartitionSpec as P

DH = 128
HALF = DH // 2
LOG2E = 1.4426950408889634
F32 = jnp.float32
BF16 = jnp.bfloat16
VMEM_BYTES = 20 * 1024 * 1024
HINT = 1_000_000_000


SMEM = pl.BlockSpec(memory_space=pltpu.SMEM)
VMEM = pl.BlockSpec(memory_space=pltpu.VMEM)
HBM = pl.BlockSpec(memory_space=pl.ANY)
FAR = pl.BlockSpec(memory_space=pltpu.HBM)


def call(kernel, name, operands, in_specs, out_shape, out_specs, scratch=(), hint=0, after=(), vmem=VMEM_BYTES):
    extra = len(after)

    def body(*refs):
        kernel(*refs[: len(operands)], *refs[len(operands) + extra :])

    return pl.pallas_call(
        body,
        in_specs=list(in_specs) + [HBM] * extra,
        out_specs=list(out_specs),
        out_shape=list(out_shape),
        scratch_shapes=list(scratch),
        compiler_params=pltpu.CompilerParams(vmem_limit_bytes=vmem),
        cost_estimate=pl.CostEstimate(flops=hint, bytes_accessed=1024, transcendentals=0),
        name=name,
    )(*operands, *after)


def run_copies(pairs, sems, first=0):
    copies = [pltpu.make_async_copy(s, d, sems.at[first + i]) for i, (s, d) in enumerate(pairs)]
    for copy in copies:
        copy.start()
    return copies


def head_columns(place, column, head):
    at = 4 * jnp.bitwise_xor(place[2], head) + column
    return pl.ds(pl.multiple_of(at * DH, DH), DH)


def block_rows(place, flip, tokens):
    return pl.ds(pl.multiple_of(jnp.bitwise_xor(place[0], flip) * tokens, tokens), tokens)


def split_kernel(place, query, key, value, out, held, sems):
    loads = run_copies([(source, held.at[index]) for index, source in enumerate((query, key, value))], sems)
    for index in range(3):
        loads[index].wait()
        for column in range(4):
            for h in range(4):
                out[column, index, :, h * DH : (h + 1) * DH] = held[index, :, head_columns(place, column, h)]


def split_heads(place, queries, keys, values, after=()):
    tokens, width = queries.shape
    out = jax.ShapeDtypeStruct((4, 3, tokens, width // 4), BF16)
    operands = (place, queries, keys, values)
    scratch = [pltpu.VMEM((3, tokens, width), BF16), pltpu.SemaphoreType.DMA((3,))]
    return call(split_kernel, "split_heads", operands, [SMEM] + [FAR] * 3, [out], [VMEM], scratch, after=after, vmem=3 * VMEM_BYTES)[0]


def chunk_kernel(place, own, got, chunk, part, sems):
    column, core = place[0], place[1]
    rows = pl.ds(pl.multiple_of((column % 2) * DH, DH), DH)
    owner = column // 2 == core
    pl.when(owner)(lambda: pltpu.make_async_copy(own.at[rows, :], chunk, sems.at[0]).start())
    pl.when(jnp.logical_not(owner))(lambda: pltpu.make_async_copy(got.at[rows, :], chunk, sems.at[0]).start())
    pltpu.make_async_copy(own.at[rows, :], chunk, sems.at[0]).wait()
    part[...] = chunk[pl.ds(pl.multiple_of(core * HALF, HALF), HALF), :]


def head_chunk(place, own, got, after=()):
    width = own.shape[1]
    out = [jax.ShapeDtypeStruct((rows, width), BF16) for rows in (DH, HALF)]
    scratch = [pltpu.SemaphoreType.DMA((1,))]
    return call(chunk_kernel, "head_chunk", (place, own, got), [SMEM, FAR, HBM], out, [VMEM] * 2, scratch, after=after)


def merge_kernel(place, blocks, *outs):
    *outs, token = outs
    token[...] = jnp.zeros_like(token)
    for column in range(4):
        for index, target in enumerate(outs):
            for h in range(4):
                target[:, head_columns(place, column, h)] = blocks[column, index, :, h * DH : (h + 1) * DH]


def merge_heads(place, blocks, after=()):
    _, _, tokens, part = blocks.shape
    out = jax.ShapeDtypeStruct((tokens, 4 * part), BF16)
    token = jax.ShapeDtypeStruct((8, DH), F32)
    return call(merge_kernel, "merge_heads", (place, blocks), [SMEM, VMEM], [out] * 3 + [token], [VMEM] * 4, after=after)


def dot(a, b, a_dim, b_dim):
    return lax.dot_general(a, b, (((a_dim,), (b_dim,)), ((), ())), preferred_element_type=F32)


def head_lanes(h):
    return pl.ds(h * DH, DH)


def load_heads(blocks, rows, sems):
    tokens = blocks.shape[2]
    return run_copies([(blocks.at[p], rows.at[:, pl.ds(p * tokens, tokens), :]) for p in range(4)], sems)


def load_pieces(pairs, sems, first, count):
    step = pairs[0][0].shape[1] // count
    copies = []
    for i in range(count):
        columns = pl.ds(i * step, step)
        copies.append(run_copies([(s.at[:, columns], d(columns)) for s, d in pairs], sems, first + i * len(pairs)))
    return copies


def cot_pairs(place, blocks, rows):
    tokens = blocks[0].shape[0]

    def target(flip, offset, count):
        start = pl.multiple_of(jnp.bitwise_xor(place[0], flip) * tokens + offset, HALF)
        return lambda columns: rows.at[pl.ds(start, count), columns]

    pairs = [(b, target(p, 0, tokens)) for p, b in enumerate(blocks[:3])]
    return pairs + [(b, target(3, i * (tokens // 2), tokens // 2)) for i, b in enumerate(blocks[3:])]


def slab_pairs(place, weights, slab):
    own, direct, crossed, half, other_half = weights
    core = place[1]

    def target(start, count):
        return lambda columns: slab.at[pl.ds(pl.multiple_of(start, HALF), count), columns]

    return [
        (own, target(0, DH)),
        (direct, target((1 + core) * DH, DH)),
        (crossed, target((2 - core) * DH, DH)),
        (half, target(3 * DH + core * HALF, HALF)),
        (other_half, target(3 * DH + (1 - core) * HALF, HALF)),
    ]


def wait_all(copies):
    for copy in copies:
        copy.wait()


def bias_rows(mask):
    rows = []
    for r in range(4):
        row = []
        for p in range(4):
            kept = mask[p * 4 + r] > 0
            row.append(jnp.full((1, DH), jnp.where(kept, 0.0, -1e30), F32))
        rows.append(jnp.concatenate(row, axis=1))
    return rows


def scores_kq(bias, query, key):
    raw = dot(key, query, 1, 1) * (LOG2E / math.sqrt(DH))
    return jnp.concatenate([raw[r * DH : (r + 1) * DH] + bias[r] for r in range(4)], axis=0)


def arrived_kernel(*refs):
    refs[-1][...] = jnp.zeros_like(refs[-1])


def arrived(arrays):
    out = jax.ShapeDtypeStruct((8, DH), F32)
    return call(arrived_kernel, "arrived", arrays, [HBM] * len(arrays), [out], [VMEM], hint=12_000_000_000)[0]


def forward_kernel(mask, blocks, attended, attended_t, log_total, qkv, sems):
    copies = load_heads(blocks, qkv, sems)
    bias = bias_rows(mask)
    wait_all(copies)
    for h in range(4):
        here = slice(h * DH, (h + 1) * DH)
        scores = scores_kq(bias, qkv[0, :, here], qkv[1, :, here])
        highest = jnp.max(scores, axis=0, keepdims=True)
        weights = jnp.exp2(scores - highest)
        total = jnp.sum(weights, axis=0, keepdims=True)
        rounded = (weights * (1.0 / total)).astype(BF16)
        out_t = dot(qkv[2, :, here], rounded, 0, 0).astype(BF16)
        attended_t[here, :] = out_t
        attended[:, here] = out_t.T
        log_total[h : h + 1, :] = highest + jnp.log2(total)


def forward(mask, blocks, after=()):
    _, _, tokens, part = blocks.shape
    length = 4 * tokens
    return call(
        forward_kernel,
        "forward",
        (mask, blocks),
        [SMEM, HBM],
        [
            jax.ShapeDtypeStruct((length, part), BF16),
            jax.ShapeDtypeStruct((part, length), BF16),
            jax.ShapeDtypeStruct((4, length), F32),
        ],
        [VMEM] * 3,
        [pltpu.VMEM((3, length, part), BF16), pltpu.SemaphoreType.DMA((4,))],
        after=after,
    )


def mixed_kernel(place, w0, w1, w2, w3, w4, attended, send_x, send_y, own, x_right, y_left, slab, total, sems):
    wait_all(load_pieces(slab_pairs(place, (w0, w1, w2, w3, w4), slab), sems, 0, 1)[0])
    tokens = attended.shape[0] // 4
    step = slab.shape[1] // 4
    for piece in range(4):
        columns = slice(piece * step, (piece + 1) * step)
        here = slice((piece % 2) * step, (piece % 2 + 1) * step)
        total[piece % 2] = dot(attended[...], slab[:, columns], 1, 0).astype(BF16)
        parts = [total.at[piece % 2][block_rows(place, flip, tokens), :] for flip in range(4)]
        own[:, columns] = parts[0]
        if piece < 2:
            send_x[0, :, here] = parts[1]
            send_x[1, :, here] = parts[3]
            y_left[:, here] = parts[2]
        else:
            send_y[0, :, here] = parts[2]
            send_y[1, :, here] = parts[3]
            x_right[:, here] = parts[1]


def mixed_parts(place, weights, attended, after=()):
    length, part = attended.shape
    width = weights[0].shape[1]
    tokens, half = length // 4, width // 2
    return call(
        mixed_kernel,
        "mixed_parts",
        (place, *weights, attended),
        [SMEM] + [HBM] * 5 + [VMEM],
        [
            jax.ShapeDtypeStruct((2, tokens, half), BF16),
            jax.ShapeDtypeStruct((2, tokens, half), BF16),
            jax.ShapeDtypeStruct((tokens, width), BF16),
            jax.ShapeDtypeStruct((tokens, half), BF16),
            jax.ShapeDtypeStruct((tokens, half), BF16),
        ],
        [VMEM] * 5,
        [
            pltpu.VMEM((part, width), BF16),
            pltpu.VMEM((2, length, width // 4), BF16),
            pltpu.SemaphoreType.DMA((5,)),
        ],
        after=after,
    )


def second_kernel(x_right, y_left, got_x, got_y, left, right):
    left[...] = (y_left[...].astype(F32) + got_x[1].astype(F32)).astype(BF16)
    right[...] = (x_right[...].astype(F32) + got_y[1].astype(F32)).astype(BF16)


def second_parts(x_right, y_left, got_x, got_y, after=()):
    out = jax.ShapeDtypeStruct(x_right.shape, BF16)
    operands = (x_right, y_left, got_x, got_y)
    return call(second_kernel, "second_parts", operands, [VMEM] * 4, [out] * 2, [VMEM] * 2, hint=HINT, after=after)


def weight_kernel(place, attended_t, c0, c1, c2, c3, c4, keep, send, cots, kept, sent, sems):
    loads = load_pieces(cot_pairs(place, (c0, c1, c2, c3, c4), cots), sems, 0, 1)[0]
    core = place[1]
    rows = []
    for half in (1 - core, core):
        for h in range(4):
            rows.append(attended_t[pl.ds(pl.multiple_of(h * DH + half * HALF, HALF), HALF), :])
    left = jnp.concatenate(rows, axis=0)
    step = cots.shape[1] // 4
    stores = []
    wait_all(loads)
    for piece in range(4):
        columns = slice(piece * step, (piece + 1) * step)
        total = dot(left, cots[:, columns], 1, 0).astype(BF16)
        for h in range(4):
            sent[h, :, columns] = total[h * HALF : (h + 1) * HALF]
            kept[h, :, columns] = total[(4 + h) * HALF : (5 + h) * HALF]
        window = pl.ds(piece * step, step)
        pairs = [(sent.at[:, :, window], send.at[:, :, window]), (kept.at[:, :, window], keep.at[:, :, window])]
        stores += run_copies(pairs, sems, 5 + 2 * piece)
    wait_all(stores)


def weight_parts(place, attended_t, cot_blocks, after=()):
    part, length = attended_t.shape
    width = cot_blocks[0].shape[1]
    out = jax.ShapeDtypeStruct((4, HALF, width), BF16)
    return call(
        weight_kernel,
        "weight_parts",
        (place, attended_t, *cot_blocks),
        [SMEM, VMEM] + [HBM] * 5,
        [out] * 2,
        [HBM] * 2,
        [
            pltpu.VMEM((length, width), BF16),
            pltpu.VMEM((4, HALF, width), BF16),
            pltpu.VMEM((4, HALF, width), BF16),
            pltpu.SemaphoreType.DMA((13,)),
        ],
        after=after,
    )


def add_kernel(keep, got, *outs):
    for h, out in enumerate(outs):
        out[...] = (keep[h].astype(F32) + got[h].astype(F32)).astype(BF16)


def add_cores(keep, got, after=()):
    out = jax.ShapeDtypeStruct(keep.shape[1:], BF16)
    return call(add_kernel, "add_cores", (keep, got), [VMEM] * 2, [out] * 4, [VMEM] * 4, after=after)


def sum_kernel(p0, p1, p2, p3, out):
    out[...] = (p0[...].astype(F32) + p1[...].astype(F32) + p2[...].astype(F32) + p3[...].astype(F32)).astype(BF16)


def sum_planes(*parts):
    out = jax.ShapeDtypeStruct(parts[0].shape, BF16)
    return call(sum_kernel, "sum_planes", parts, [VMEM] * 4, [out], [VMEM], hint=0)[0]


def weight_out_kernel(place, p0, p1, p2, p3, out, held, sems):
    copies = []
    for k, piece in enumerate((p0, p1, p2, p3)):
        head = jnp.bitwise_xor(place[0] % 2, k % 2)
        half = jnp.bitwise_xor(jnp.bitwise_xor(place[1], place[0] // 2), k // 2)
        start = pl.multiple_of(head * DH + half * HALF, HALF)
        held[k] = piece[...].astype(F32) * 0.125
        copies += run_copies([(held.at[k], out.at[pl.ds(start, HALF), :])], sems, k)
    wait_all(copies)


def weight_out(place, pieces, after=()):
    rows, width = pieces[0].shape
    out = jax.ShapeDtypeStruct((4 * rows, width), F32)
    scratch = [pltpu.VMEM((4, rows, width), F32), pltpu.SemaphoreType.DMA((4,))]
    return call(weight_out_kernel, "weight_out", (place, *pieces), [SMEM] + [VMEM] * 4, [out], [HBM], scratch, after=after)[0]


def grads_kernel(place, w0, w1, w2, w3, w4, c0, c1, c2, c3, c4, grads, slab, cots, sems):
    loads = load_pieces(slab_pairs(place, (w0, w1, w2, w3, w4), slab), sems, 0, 1)
    loads += load_pieces(cot_pairs(place, (c0, c1, c2, c3, c4), cots), sems, 5, 1)
    wait_all(loads[0] + loads[1])
    for pair in range(2):
        rows = slice(pair * 2 * DH, (pair + 1) * 2 * DH)
        grads[:, rows] = dot(cots[...], slab[rows, :], 1, 1).astype(BF16)


def attended_grads(place, weights, cot_blocks, after=()):
    tokens, width = cot_blocks[0].shape
    part, length = 4 * DH, 4 * tokens
    return call(
        grads_kernel,
        "attended_grads",
        (place, *weights, *cot_blocks),
        [SMEM] + [HBM] * 10,
        [jax.ShapeDtypeStruct((length, part), BF16)],
        [VMEM],
        [
            pltpu.VMEM((part, width), BF16),
            pltpu.VMEM((length, width), BF16),
            pltpu.SemaphoreType.DMA((10,)),
        ],
        after=after,
    )[0]


def backward_kernel(mask, log_total, grads, blocks, out, qkv, made, sems):
    loads = load_heads(blocks, qkv, sems)
    tokens = out.shape[2]
    scale = 1.0 / math.sqrt(DH)
    bias = bias_rows(mask)
    stores = []
    wait_all(loads)
    for h in range(4):
        here = slice(h * DH, (h + 1) * DH)
        query, key, value, grad = qkv[0, :, here], qkv[1, :, here], qkv[2, :, here], grads[:, here]
        probs = jnp.exp2(scores_kq(bias, query, key) - log_total[h : h + 1, :])
        grad_value = dot(probs.astype(BF16), grad, 1, 0).astype(BF16)
        grad_probs = dot(value, grad, 1, 1)
        delta = jnp.sum(probs * grad_probs, axis=0, keepdims=True)
        grad_scores = (probs * (grad_probs - delta) * scale).astype(BF16)
        grad_key = dot(grad_scores, query, 1, 0).astype(BF16)
        grad_query = dot(key, grad_scores, 0, 0).astype(BF16).T
        for index, full in enumerate((grad_query, grad_key, grad_value)):
            for p in range(4):
                made[p, index, :, here] = full[p * tokens : (p + 1) * tokens]
        stores += run_copies([(made.at[:, :, :, head_lanes(h)], out.at[:, :, :, head_lanes(h)])], sems, 4 + h)
    wait_all(stores)


def backward(mask, log_total, grads, blocks, after=()):
    _, _, tokens, part = blocks.shape
    length = 4 * tokens
    return call(
        backward_kernel,
        "backward",
        (mask, log_total, grads, blocks),
        [SMEM] + [VMEM] * 2 + [HBM],
        [jax.ShapeDtypeStruct(blocks.shape, BF16)],
        [HBM],
        [pltpu.VMEM((3, length, part), BF16), pltpu.VMEM(blocks.shape, BF16), pltpu.SemaphoreType.DMA((8,))],
        after=after,
    )[0]


def column_shards(queries, keys, values, out_weight, cotangent, block_mask):
    tokens, width = queries.shape[1:]
    column = lax.axis_index("seq")
    rank = lax.axis_index("dp")
    core, z = rank % 2, rank // 2
    place = jnp.stack([column, core, z]).astype(jnp.int32)
    mask = block_mask.reshape(-1)
    cot = cotangent[0]

    def plane(array, flip):
        return lax.ppermute(array, "seq", [(i, i ^ flip) for i in range(4)])

    def swap(array):
        return lax.ppermute(array, "dp", [(i, i ^ 1) for i in range(8)])

    def along(array, flip):
        return lax.ppermute(array, "dp", [(i, i ^ (2 * flip)) for i in range(8)])

    def columns(array):
        return lax.all_to_all(array, "seq", 0, 0, tiled=True)

    heads = split_heads(place, queries[0], keys[0], values[0])
    blocks = columns(heads)

    cot_x, cot_y = plane(cot, 1), plane(cot, 2)

    def in_dp(array, target):
        return lax.ppermute(array, "dp", [(2 * a + c, target(a, c)) for a in range(4) for c in range(2)])

    chunk, part = head_chunk(place, out_weight, swap(out_weight), after=(heads,))
    direct = in_dp(chunk, lambda a, c: 2 * (a ^ (1 + c)) + c)
    part = in_dp(part, lambda a, c: 2 * (a ^ 3) + c)

    half = tokens // 2
    cot_blocks = (cot, cot_x, cot_y, plane(cot_y[:half], 1), plane(cot_x[half:], 2))
    attended, attended_t, log_total = forward(mask, blocks, after=(arrived((cot_x, cot_y)),))

    crossed, other, attended = lax.optimization_barrier((swap(direct), swap(part), attended))
    weights = (chunk, direct, crossed, part, other)

    send_x, send_y, mixed_own, x_right, y_left = mixed_parts(place, weights, attended)
    got_x, got_y = plane(send_x, 1), plane(send_y, 2)

    keep, send = weight_parts(place, attended_t, cot_blocks, after=(send_x,))
    grads = attended_grads(place, weights, cot_blocks, after=(keep,))
    s0, s1, s2, s3 = add_cores(keep, swap(send), after=(grads,))
    got = [along(s, flip).astype(F32) for flip, s in ((1, s1), (2, s2), (3, s3))]
    summed = (s0.astype(F32) + got[0] + got[1] + got[2]).astype(BF16)
    made = backward(mask, log_total, grads, blocks, after=(s1,))
    outs = columns(made)
    left, right = second_parts(x_right, y_left, got_x, got_y, after=(made,))
    got_left, got_right = plane(left, 2), plane(right, 1)
    mixed = jnp.concatenate(
        [
            mixed_own[:, : width // 2].astype(F32) + got_x[0].astype(F32) + got_left.astype(F32),
            mixed_own[:, width // 2 :].astype(F32) + got_y[0].astype(F32) + got_right.astype(F32),
        ],
        axis=1,
    ).astype(BF16)

    pieces = []
    for k in range(4):
        pairs = []
        for plane_at in range(4):
            for c in range(2):
                for t in range(4):
                    to_core, to_column = t // 2, t ^ (2 * c) ^ k
                    pairs.append(((2 * plane_at + c) * 4 + t, (2 * plane_at + to_core) * 4 + to_column))
        pieces.append(lax.ppermute(summed, ("dp", "seq"), pairs))
    *merged, token = merge_heads(place, outs, after=(summed, mixed))
    grad_weight = weight_out(place, pieces, after=(token,))
    return (mixed[None],) + tuple(g[None] for g in merged) + (grad_weight,)


def attend(query_heads, key_heads, value_heads, grad_heads, block_mask):
    batch, length, width = query_heads.shape
    heads = width // DH
    shape_split = (batch, length, heads, DH)
    query_split = query_heads.reshape(shape_split)
    key_split = key_heads.reshape(shape_split)
    value_split = value_heads.reshape(shape_split)
    grad_split = grad_heads.reshape(shape_split)
    block = length // block_mask.shape[2]
    rows_step = min(512, length)
    scale = 1.0 / math.sqrt(DH)

    def step(carry, index):
        key_total, value_total = carry
        start = index * rows_step
        query_part = lax.dynamic_slice_in_dim(query_split, start, rows_step, 1)
        grad_part = lax.dynamic_slice_in_dim(grad_split, start, rows_step, 1)
        mask_part = lax.dynamic_slice_in_dim(block_mask, start // block, rows_step // block, 1)
        allowed = jnp.repeat(jnp.repeat(mask_part, block, axis=1), block, axis=2) > 0
        scores = (
            jnp.einsum("bqhd,bkhd->bhqk", query_part, key_split, preferred_element_type=jnp.float32)
            * scale
        )
        scores = jnp.where(allowed[:, None], scores, -1e30)
        highest = jnp.max(scores, axis=3, keepdims=True)
        log_total = highest + jnp.log(jnp.sum(jnp.exp(scores - highest), axis=3, keepdims=True))
        probs = jnp.exp(scores - log_total)
        rounded = probs.astype(jnp.bfloat16)
        attended = jnp.einsum(
            "bhqk,bkhd->bqhd", rounded, value_split, preferred_element_type=jnp.float32
        ).astype(jnp.bfloat16)
        value_total = value_total + jnp.einsum(
            "bhqk,bqhd->bkhd", rounded, grad_part, preferred_element_type=jnp.float32
        )
        grad_probs = jnp.einsum(
            "bqhd,bkhd->bhqk", grad_part, value_split, preferred_element_type=jnp.float32
        )
        delta = jnp.sum(probs * grad_probs, axis=3, keepdims=True)
        grad_scores = (probs * (grad_probs - delta) * scale).astype(jnp.bfloat16)
        grad_query = jnp.einsum(
            "bhqk,bkhd->bqhd", grad_scores, key_split, preferred_element_type=jnp.float32
        ).astype(jnp.bfloat16)
        key_total = key_total + jnp.einsum(
            "bhqk,bqhd->bkhd", grad_scores, query_part, preferred_element_type=jnp.float32
        )
        return ((key_total, value_total), (attended, grad_query))

    zeros = jnp.zeros(shape_split, jnp.float32)
    totals, pieces = lax.scan(
        step, (zeros, zeros), jnp.arange(length // rows_step, dtype=jnp.int32)
    )

    def joined(parts):
        return jnp.moveaxis(parts, 0, 1).reshape(batch, length, width)

    grad_key = totals[0].astype(jnp.bfloat16).reshape(batch, length, width)
    grad_value = totals[1].astype(jnp.bfloat16).reshape(batch, length, width)
    return (joined(pieces[0]), joined(pieces[1]), grad_key, grad_value)


def general_shards(queries, keys, values, out_weight, cotangent, block_mask):
    batch, tokens, width = queries.shape
    query_heads, key_heads, value_heads = (
        lax.all_to_all(queries, "seq", split_axis=2, concat_axis=1, tiled=True),
        lax.all_to_all(keys, "seq", split_axis=2, concat_axis=1, tiled=True),
        lax.all_to_all(values, "seq", split_axis=2, concat_axis=1, tiled=True),
    )
    weight_full = lax.all_gather(out_weight, "dp", axis=0, tiled=True)
    flat_cot = cotangent.reshape(batch * tokens, width)
    grad_attn = lax.dot_general(
        flat_cot, weight_full, (((1,), (1,)), ((), ())), preferred_element_type=jnp.float32
    )
    grad_attn = grad_attn.astype(jnp.bfloat16).reshape(batch, tokens, width)
    grad_heads = lax.all_to_all(grad_attn, "seq", split_axis=2, concat_axis=1, tiled=True)
    attended_heads, grad_q_heads, grad_k_heads, grad_v_heads = attend(
        query_heads, key_heads, value_heads, grad_heads, block_mask
    )
    attended, grad_queries, grad_keys, grad_values = (
        lax.all_to_all(attended_heads, "seq", split_axis=1, concat_axis=2, tiled=True),
        lax.all_to_all(grad_q_heads, "seq", split_axis=1, concat_axis=2, tiled=True),
        lax.all_to_all(grad_k_heads, "seq", split_axis=1, concat_axis=2, tiled=True),
        lax.all_to_all(grad_v_heads, "seq", split_axis=1, concat_axis=2, tiled=True),
    )
    flat_att = attended.reshape(batch * tokens, width)
    mixed = (
        jnp.dot(flat_att, weight_full, preferred_element_type=jnp.float32)
        .astype(jnp.bfloat16)
        .reshape(batch, tokens, width)
    )
    partial_grad = lax.psum_scatter(
        lax.dot_general(
            flat_att, flat_cot, (((0,), (0,)), ((), ())), preferred_element_type=jnp.float32
        ),
        "dp",
        scatter_dimension=0,
        tiled=True,
    )
    summed = lax.psum(partial_grad, "seq")
    grad_weight = summed / (batch * lax.axis_size("dp"))
    return (mixed, grad_queries, grad_keys, grad_values, grad_weight)


def fits_columns(mesh, queries, out_weight, block_mask):
    batch, length, width = queries
    return (
        mesh.shape["dp"] == 8
        and mesh.shape["seq"] == 4
        and batch == 8
        and length == 4 * DH
        and width == 16 * DH
        and out_weight == (width, width)
        and block_mask == (batch, 4, 4)
    )


def solution(mesh):
    placed = (
        P("dp", "seq", None),
        P("dp", "seq", None),
        P("dp", "seq", None),
        P("dp", None),
        P("dp", "seq", None),
        P("dp", None, None),
    )

    def program(queries, keys, values, out_weight, cotangent, block_mask):
        fits = fits_columns(mesh, queries.shape, out_weight.shape, block_mask.shape)
        return jax.shard_map(
            column_shards if fits else general_shards,
            mesh=mesh,
            in_specs=placed,
            out_specs=(
                P("dp", "seq", None),
                P("dp", "seq", None),
                P("dp", "seq", None),
                P("dp", "seq", None),
                P("dp", None),
            ),
            check_vma=False,
        )(queries, keys, values, out_weight, cotangent, block_mask)

    return program
```
